128 devices in a mesh: dp: 8 (over x_lo, y), tensor: 16 (over z, x_hi, core).
Axes of the slice: x: 4 (x_hi: 2, x_lo: 2; x = x_hi * 2 + x_lo), y: 4, z: 4, core: 2. Of those that a mesh axis runs over, the one named last changes fastest.
Arguments:
- hidden: bfloat16 [2, 64, 8192], P(None, 'dp'), may hold values from -6 to 6
- norm_gain: bfloat16 [8192], replicated, may hold values from 0.099609375 to 1.8984375
- qkv_bias: bfloat16 [5120], P('tensor'), may hold values from -16 to 16
- key_cache: bfloat16 [64, 4096, 512], P('dp', 'tensor'), may hold values from -18 to 18
- value_cache: bfloat16 [64, 4096, 512], P('dp', 'tensor'), may hold values from -6 to 6
- lengths: int32 [64], P('dp'), may hold values from 2 to 4094, as said below
- fresh_qkv: bfloat16 [8192, 5120], P(('dp', 'tensor')), may hold values from -0.0625 to 0.0625
- fresh_out: bfloat16 [8192, 4096], P(('dp', 'tensor')), may hold values from -0.1875 to 0.1875
Outputs:
- attn_output: bfloat16 [2, 64, 8192], P(None, 'dp', 'tensor')
- grouped_qkv: bfloat16 [8192, 5120], P(None, 'tensor')
- grouped_out: bfloat16 [8192, 4096], P(None, 'tensor')
The draws below stay inside these ranges and needn't reach their ends.
Inputs may be any that keep to these rules, and one draw needn't show every extreme that they name: `lengths`: each request has at least 2 cached positions; in every block of 8 requests one has 4094 and one has 2.
All inputs are finite; a program needn't handle non-finite values.
Results may differ from the reference program's by a relative error of at most 0.027.
Values may be sent and summed in bfloat16 or wider, within the bound.
No kernel may reach another device: no remote copies, remote signals or barrier semaphores. Data moves between devices by JAX's collectives and lax.ppermute only.
A program may use at most 128 MiB of HBM per device.

```python
import math
import jax
import jax.numpy as jnp
from jax import lax

D = 8192
HD = 128
QH = 32
KVH = 4
CACHE = 4096
STEPS = 2
ROWS_REP = 8
ROWS = 64
QW = 4096
QKV = 5120
N_TENSOR = 16


def draw_qkv_bias(key, part):
    key = jax.random.fold_in(key, 11)
    noise = jnp.clip(jax.random.normal(key, (QH * HD + 2 * KVH * HD,), jnp.float32), -6.0, 6.0)
    natural = noise
    query_part = natural[:QH * HD].reshape(N_TENSOR, -1)
    key_part = natural[QH * HD:QH * HD + KVH * HD].reshape(N_TENSOR, -1)
    value_part = natural[QH * HD + KVH * HD:].reshape(N_TENSOR, -1)
    return jnp.concatenate([query_part, key_part, value_part], 1).reshape(-1).astype(jnp.bfloat16)


def draw_key_cache(key, part):
    key = jax.random.fold_in(key, 12)
    gaussian = jnp.clip(jax.random.normal(key, (ROWS, CACHE, KVH, HD), jnp.float32), -6.0, 6.0)
    result = 1.4 * gaussian
    return result.reshape(ROWS, CACHE, KVH * HD).astype(jnp.bfloat16)


def draw_lengths(key, part):
    key = jax.random.fold_in(key, 13)
    first_key, second_key = jax.random.split(key)
    top_exponent = CACHE.bit_length() - 1
    exponent = jax.random.randint(first_key, (ROWS,), 1, top_exponent)
    lower = jnp.left_shift(jnp.ones((ROWS,), jnp.int32), exponent)
    drawn = jax.random.randint(second_key, (ROWS,), lower, 2 * lower)
    drawn = jnp.minimum(drawn, CACHE - 2)
    slot_ids = jnp.arange(ROWS) % ROWS_REP
    return jnp.where(slot_ids == 0, CACHE - 2, jnp.where(slot_ids == 1, 2, drawn)).astype(jnp.int32)


def level_of(own_key, extent, cuts, least, top_value):
    loudness = 1.0
    for axis_at, blocks in cuts:
        heights = jax.random.uniform(jax.random.fold_in(jax.random.fold_in(own_key, 6), axis_at), (blocks,), jnp.float32, least / len(cuts), top_value / len(cuts))
        loudness = loudness * jnp.repeat(jnp.exp(heights), extent[axis_at] // blocks).reshape((-1,) + (1,) * (len(extent) - 1 - axis_at))
    return loudness


def bell_draw(stream_key, dims, spread, limit, cuts=(), held_as=jnp.bfloat16):
    factor_of = level_of(stream_key, dims, cuts, -0.22, 0.18) if cuts else 1.0
    entries = jax.random.normal(stream_key, dims, jnp.float32) * spread * factor_of
    return jnp.minimum(jnp.maximum(entries, -limit), limit).astype(held_as)


def setup_inputs(seed: int = 0) -> dict:
    keys = jax.random.split(jax.random.key(seed), 9)
    return {
        "hidden": bell_draw(keys[0], (STEPS, ROWS, D), 1.0, 6.0, ((1, 8),)),
        "norm_gain": jnp.clip(1.0 + 0.18 * jax.random.normal(keys[1], (D,), jnp.float32), 0.099609375, 1.8984375).astype(jnp.bfloat16),
        "qkv_bias": draw_qkv_bias(jax.random.fold_in(keys[8], 71), 0),
        "key_cache": draw_key_cache(jax.random.fold_in(keys[8], 71), 0),
        "value_cache": bell_draw(keys[4], (ROWS, CACHE, KVH * HD), 1.0, 6.0, ((0, 8), (1, 16))),
        "lengths": draw_lengths(jax.random.fold_in(keys[8], 71), 0),
        "fresh_qkv": bell_draw(keys[6], (D, QKV), D ** -0.5, 0.0625, ((0, 128),)),
        "fresh_out": bell_draw(keys[7], (D, QW), (8 * HD) ** -0.5, 0.1875, ((0, 128),)),
    }


THETA = 1000000.0
EPS = 1e-06

def rotate(values, position):
    full_width = values.shape[-1]
    half_width = full_width // 2
    inverse = THETA ** (-jnp.arange(half_width, dtype=jnp.float32) * 2.0 / full_width)
    angles = position[..., None] * inverse
    cosine = jnp.cos(angles)
    sine_part = jnp.sin(angles)
    cosine = jnp.concatenate([cosine, cosine], -1)
    sine_part = jnp.concatenate([sine_part, sine_part], -1)
    turned = jnp.concatenate([-values[..., half_width:], values[..., :half_width]], -1)
    return values * cosine + turned * sine_part

def regroup_columns(natural):
    row_count = natural.shape[0]
    query_part = natural[:, :QH * HD].reshape(row_count, N_TENSOR, -1)
    key_part = natural[:, QH * HD:QH * HD + KVH * HD].reshape(row_count, N_TENSOR, -1)
    value_part = natural[:, QH * HD + KVH * HD:].reshape(row_count, N_TENSOR, -1)
    return jnp.concatenate([query_part, key_part, value_part], 2).reshape(row_count, -1)

def reference(hidden, norm_gain, qkv_bias, key_cache, value_cache, lengths, fresh_qkv, fresh_out):
    grouped_qkv = regroup_columns(fresh_qkv)
    states = hidden.astype(jnp.float32)
    normed = states * lax.rsqrt(lax.optimization_barrier(jnp.mean(states * states, -1, keepdims=True)) + EPS) * norm_gain.astype(jnp.float32)
    normed = normed.astype(jnp.bfloat16).reshape(STEPS * ROWS, D)
    projected = jnp.dot(normed, grouped_qkv, preferred_element_type=jnp.float32) + qkv_bias.astype(jnp.float32)
    grouped = projected.astype(jnp.bfloat16).reshape(STEPS, ROWS, N_TENSOR, -1)
    query_width = QH * HD // N_TENSOR
    kv_width = KVH * HD // N_TENSOR
    queries = grouped[..., :query_width].reshape(STEPS, ROWS, QH, HD)
    new_keys = grouped[..., query_width:query_width + kv_width].reshape(STEPS, ROWS, KVH, HD)
    new_values = grouped[..., query_width + kv_width:].reshape(STEPS, ROWS, KVH, HD)
    position = (lengths[None, :] + jnp.arange(STEPS, dtype=jnp.int32)[:, None]).astype(jnp.float32)[:, :, None]
    queries = rotate(queries.astype(jnp.float32), position).astype(jnp.bfloat16)
    new_keys = rotate(new_keys.astype(jnp.float32), position).astype(jnp.bfloat16)
    score_scale = 1.0 / math.sqrt(HD)
    per_kv = QH // KVH

    def one_row(row_items):
        row_queries, row_keys, row_values, cache_keys, cache_values, row_length = row_items
        cache_keys = cache_keys.reshape(CACHE, KVH, HD).astype(jnp.float32)
        cache_values = cache_values.reshape(CACHE, KVH, HD).astype(jnp.float32)
        grouped_queries = row_queries.reshape(STEPS, KVH, per_kv, HD).astype(jnp.float32)
        scores = jnp.einsum('skgd,pkd->skgp', grouped_queries, cache_keys) * score_scale
        valid_mask = jnp.arange(CACHE, dtype=jnp.int32) < row_length
        scores = jnp.where(valid_mask, scores, -jnp.inf)
        fresh_scores = jnp.einsum('skgd,tkd->skgt', grouped_queries, row_keys.astype(jnp.float32)) * score_scale
        causal = (jnp.arange(STEPS)[None, :] <= jnp.arange(STEPS)[:, None])[:, None, None, :]
        fresh_scores = jnp.where(causal, fresh_scores, -jnp.inf)
        best_score = jnp.maximum(lax.optimization_barrier(jnp.max(scores, -1)), lax.optimization_barrier(jnp.max(fresh_scores, -1)))
        cache_weights = jnp.exp(scores - best_score[..., None])
        fresh_weights = jnp.exp(fresh_scores - best_score[..., None])
        totals = lax.optimization_barrier(jnp.sum(cache_weights, -1)) + lax.optimization_barrier(jnp.sum(fresh_weights, -1))
        mixture = jnp.einsum('skgp,pkd->skgd', cache_weights.astype(jnp.bfloat16).astype(jnp.float32), cache_values)
        mixture = mixture + jnp.einsum('skgt,tkd->skgd', fresh_weights.astype(jnp.bfloat16).astype(jnp.float32), row_values.astype(jnp.float32))
        return (mixture / totals[..., None]).reshape(STEPS, QH * HD)
    attended = lax.map(one_row, (queries.transpose(1, 0, 2, 3), new_keys.transpose(1, 0, 2, 3), new_values.transpose(1, 0, 2, 3), key_cache, value_cache, lengths))
    attended = attended.transpose(1, 0, 2).astype(jnp.bfloat16).reshape(STEPS * ROWS, QH * HD)
    attn_output = jnp.dot(attended, fresh_out.T, preferred_element_type=jnp.float32).astype(jnp.bfloat16).reshape(STEPS, ROWS, D)
    return (attn_output, grouped_qkv, fresh_out)
```

```python
import math

import jax
import jax.numpy as jnp
from jax import lax
from jax.sharding import PartitionSpec as P

HD = 128
QH = 32
KVH = 4
THETA = 1000000.0
EPS = 1e-06
FLOOR = -1e30


def rotate(values, position):
    full_width = values.shape[-1]
    half_width = full_width // 2
    inverse = THETA ** (-jnp.arange(half_width, dtype=jnp.float32) * 2.0 / full_width)
    angles = position[..., None] * inverse
    cosine = jnp.cos(angles)
    sine_part = jnp.sin(angles)
    cosine = jnp.concatenate([cosine, cosine], -1)
    sine_part = jnp.concatenate([sine_part, sine_part], -1)
    turned = jnp.concatenate([-values[..., half_width:], values[..., :half_width]], -1)
    return values * cosine + turned * sine_part


def column_groups(natural, groups):
    row_count = natural.shape[0]
    query_part = natural[:, : QH * HD].reshape(row_count, groups, -1)
    key_part = natural[:, QH * HD : QH * HD + KVH * HD].reshape(row_count, groups, -1)
    value_part = natural[:, QH * HD + KVH * HD :].reshape(row_count, groups, -1)
    return jnp.concatenate([query_part, key_part, value_part], 2).transpose(1, 0, 2)


def exchange(blocks, axis):
    return lax.all_to_all(blocks, axis, split_axis=0, concat_axis=0, tiled=True)


def two_halves(value):
    upper = lax.reduce_precision(value, 8, 7)
    return upper, lax.reduce_precision(value - upper, 8, 7)


def on_device(hidden, norm_gain, qkv_bias, key_cache, value_cache, lengths, fresh_qkv, fresh_out):
    groups = lax.axis_size("tensor")
    member = lax.axis_index("tensor")
    replicas = lax.axis_size("dp")
    step_count, row_count, feature_width = hidden.shape
    slots = step_count * row_count
    share = feature_width // replicas
    query_width = QH * HD // groups
    kv_width = KVH * HD // groups
    own_heads = QH // groups
    per_kv = QH // KVH
    score_scale = 1.0 / math.sqrt(HD)

    own_qkv = exchange(column_groups(fresh_qkv, groups), "tensor").reshape(share, -1)
    own_out = exchange(
        fresh_out.reshape(fresh_out.shape[0], groups, -1).transpose(1, 0, 2), "tensor"
    ).reshape(share, -1)

    states = hidden.astype(jnp.float32)
    normed = (
        states
        * lax.rsqrt(jnp.mean(states * states, -1, keepdims=True) + EPS)
        * norm_gain.astype(jnp.float32)
    )
    normed = normed.astype(jnp.bfloat16).reshape(slots, replicas, share).transpose(1, 0, 2)
    all_normed = exchange(normed, "dp").reshape(replicas * slots, share)

    grouped_out = lax.all_gather(own_out, "dp", axis=0, tiled=True)
    grouped_qkv = lax.all_gather(own_qkv.T, "dp", axis=1, tiled=True).T

    terms = jnp.dot(all_normed, own_qkv, preferred_element_type=jnp.float32)
    terms = exchange(terms.reshape(replicas, slots, -1), "dp")
    projected = (jnp.sum(terms, 0) + qkv_bias.astype(jnp.float32)).astype(jnp.bfloat16)
    gathered = exchange(jnp.broadcast_to(projected[None], (groups,) + projected.shape), "tensor")

    grouped = gathered.reshape(groups, step_count, row_count, -1).transpose(1, 2, 0, 3)
    queries = grouped[..., :query_width].reshape(step_count, row_count, QH, HD)
    new_keys = grouped[..., query_width : query_width + kv_width].reshape(
        step_count, row_count, KVH, HD
    )
    new_values = grouped[..., query_width + kv_width :].reshape(step_count, row_count, KVH, HD)
    position = (lengths[None, :] + jnp.arange(step_count, dtype=jnp.int32)[:, None]).astype(
        jnp.float32
    )[:, :, None]
    queries = rotate(queries.astype(jnp.float32), position).astype(jnp.bfloat16)
    new_keys = rotate(new_keys.astype(jnp.float32), position).astype(jnp.bfloat16)

    cache_span = key_cache.shape[1]
    offset = member * cache_span
    valid_rows = (offset + jnp.arange(cache_span, dtype=jnp.int32))[None, :] < lengths[:, None]
    valid_mask = valid_rows[None, :, None, None, :]
    cache_keys = key_cache.reshape(row_count, cache_span, KVH, HD)
    cache_values = value_cache.reshape(row_count, cache_span, KVH, HD)
    grouped_queries = queries.reshape(step_count, row_count, KVH, per_kv, HD)
    scores = (
        jnp.einsum(
            "srkgd,rpkd->srkgp", grouped_queries, cache_keys, preferred_element_type=jnp.float32
        )
        * score_scale
    )
    scores = jnp.where(valid_mask, scores, FLOOR)
    highest_upper, highest_lower = two_halves(jnp.max(scores, -1))
    highest = highest_upper + highest_lower
    weights = jnp.where(valid_mask, jnp.exp(scores - highest[..., None]), 0.0)
    totals_upper, totals_lower = two_halves(jnp.sum(weights, -1))
    partial_value = jnp.einsum(
        "srkgp,rpkd->srkgd",
        weights.astype(jnp.bfloat16),
        cache_values,
        preferred_element_type=jnp.float32,
    )

    def by_head(part):
        return part.reshape(slots, groups, own_heads, -1).transpose(1, 0, 2, 3)

    facts = jnp.concatenate(
        [
            by_head(part).reshape(groups, 1, slots * own_heads)
            for part in (highest_upper, highest_lower, totals_upper, totals_lower)
        ],
        2,
    )
    message = jnp.concatenate(
        [
            by_head(partial_value).astype(jnp.bfloat16).reshape(groups, slots * own_heads, HD),
            facts.astype(jnp.bfloat16),
        ],
        1,
    )
    message = exchange(message, "tensor")
    parts = message[:, : slots * own_heads].astype(jnp.float32)
    facts = message[:, slots * own_heads].astype(jnp.float32).reshape(groups, 4, slots * own_heads)
    highest = facts[:, 0] + facts[:, 1]
    totals = facts[:, 2] + facts[:, 3]

    head_start = member * own_heads
    own_queries = lax.dynamic_slice_in_dim(queries, head_start, own_heads, 2)
    kv_index = head_start // per_kv
    own_keys = lax.dynamic_slice_in_dim(new_keys, kv_index, 1, 2)[:, :, 0]
    own_values = lax.dynamic_slice_in_dim(new_values, kv_index, 1, 2)[:, :, 0]
    fresh_scores = (
        jnp.einsum("srhd,trd->srht", own_queries, own_keys, preferred_element_type=jnp.float32)
        * score_scale
    )
    causal = (jnp.arange(step_count)[None, :] <= jnp.arange(step_count)[:, None])[:, None, None, :]
    fresh_scores = jnp.where(causal, fresh_scores, FLOOR).reshape(slots * own_heads, step_count)
    best_score = jnp.maximum(jnp.max(highest, 0), jnp.max(fresh_scores, -1))
    rescale = jnp.exp(highest - best_score)
    fresh_weights = jnp.exp(fresh_scores - best_score[:, None])
    totals = jnp.sum(totals * rescale, 0) + jnp.sum(fresh_weights, -1)
    mixture = jnp.sum(parts * rescale[..., None], 0) + jnp.einsum(
        "srht,trd->srhd",
        fresh_weights.astype(jnp.bfloat16).reshape(step_count, row_count, own_heads, step_count),
        own_values,
        preferred_element_type=jnp.float32,
    ).reshape(slots * own_heads, HD)
    attended = (mixture / totals[:, None]).astype(jnp.bfloat16).reshape(slots, own_heads * HD)

    term_sums = jnp.dot(attended, grouped_out.T, preferred_element_type=jnp.float32)
    term_sums = term_sums.astype(jnp.bfloat16).reshape(slots, groups, -1).transpose(1, 0, 2)
    attn_output = jnp.sum(exchange(term_sums, "tensor").astype(jnp.float32), 0)
    attn_output = attn_output.astype(jnp.bfloat16).reshape(step_count, row_count, -1)
    return (attn_output, grouped_qkv, grouped_out)


def solution(mesh):
    return jax.shard_map(
        on_device,
        mesh=mesh,
        in_specs=(
            P(None, "dp", None),
            P(),
            P("tensor"),
            P("dp", "tensor", None),
            P("dp", "tensor", None),
            P("dp"),
            P(("dp", "tensor"), None),
            P(("dp", "tensor"), None),
        ),
        out_specs=(P(None, "dp", "tensor"), P(None, "tensor"), P(None, "tensor")),
        check_vma=False,
    )
```

```python
import math

import jax
import jax.numpy as jnp
from jax import lax
from jax.experimental import pallas as pl
from jax.experimental.pallas import tpu as pltpu
from jax.sharding import PartitionSpec as P

HD = 128
QH = 32
KVH = 4
THETA = 1000000.0
EPS = 1e-06
FLOOR = -1e30


def pack_kernel(groups, spot_ref, states_ref, gain_ref, qkv_ref, out_ref, packed_ref, own_ref, send_ref):
    query_width = QH * HD // groups
    kv_width = KVH * HD // groups
    rows = qkv_ref.shape[0]
    for g in range(groups):
        keys_at = QH * HD + g * kv_width
        values_at = QH * HD + KVH * HD + g * kv_width
        packed_ref[g, :, :query_width] = qkv_ref[:, g * query_width : (g + 1) * query_width]
        packed_ref[g, :, query_width : query_width + HD] = jnp.concatenate(
            [
                qkv_ref[:, keys_at : keys_at + kv_width],
                qkv_ref[:, values_at : values_at + kv_width],
                jnp.zeros((rows, HD - 2 * kv_width), qkv_ref.dtype),
            ],
            1,
        )
        packed_ref[g, :, query_width + HD :] = out_ref[:, g * query_width : (g + 1) * query_width]
    states = states_ref[...].astype(jnp.float32)
    normed = (
        states
        * lax.rsqrt(jnp.mean(states * states, -1, keepdims=True) + EPS)
        * gain_ref[...].astype(jnp.float32)
    ).astype(jnp.bfloat16)
    column, y_at = spot_ref[0], spot_ref[1]
    count, _, share = own_ref.shape
    for y in range(count):
        first = normed[:, y * share : (y + 1) * share]
        second = normed[:, (count + y) * share : (count + y + 1) * share]
        slot = (y - y_at) & 3
        own_ref[slot] = jnp.where(column == 0, first, second)
        send_ref[slot] = jnp.where(column == 0, second, first)


def terms_kernel(group_width, order_ref, own, got, low, high, far, packed_ref, terms_ref, out_ref):
    weights = packed_ref[:, :group_width]
    states = jnp.concatenate(
        [own[0], got[0], low[0], low[1], high[0], high[1], far[0], far[1]], 0
    )
    terms = jnp.dot(states, weights, preferred_element_type=jnp.float32)
    slots = own.shape[1]
    for i in range(terms.shape[0] // slots):
        terms_ref[order_ref[i]] = terms[i * slots : (i + 1) * slots]
    out_ref[...] = packed_ref[:, group_width + 64 :]


def hold_kernel(*refs):
    pass


def hold(*values):
    anywhere = pl.BlockSpec(memory_space=pl.ANY)
    return pl.pallas_call(
        hold_kernel,
        out_shape=tuple(jax.ShapeDtypeStruct(v.shape, v.dtype) for v in values),
        in_specs=[anywhere] * len(values),
        out_specs=(anywhere,) * len(values),
        input_output_aliases={i: i for i in range(len(values))},
        name="hold",
    )(*values)


def sum_kernel(groups, terms_ref, bias_ref, *refs):
    projected_ref = refs[4]
    total = jnp.sum(terms_ref[...], 0) + bias_ref[...].astype(jnp.float32)
    total = total.astype(projected_ref.dtype)
    for g in range(groups):
        projected_ref[g] = total


def turn_kernel(packed_ref, turned_ref):
    width = turned_ref.shape[0]
    turned_ref[...] = packed_ref[:, : width + 64].T[:width]


def place_kernel(axis, count, *refs):
    starts_ref, parts, whole_ref, sems = refs[0], refs[1 : 1 + count], refs[-2], refs[-1]
    pieces = sems.shape[1]
    copies = []
    for i, part in enumerate(parts):
        rows, columns = part.shape
        step = rows // pieces
        at = pl.multiple_of(starts_ref[i] * 512, 512)
        for j in range(pieces):
            if axis == 0:
                target = whole_ref.at[pl.ds(at + j * step, step), :]
            else:
                target = whole_ref.at[pl.ds(j * step, step), pl.ds(at, columns)]
            source = part.at[pl.ds(j * step, step), :]
            copies.append(pltpu.make_async_copy(source, target, sems.at[i, j]))
    for copy in copies:
        copy.start()
    for copy in copies:
        copy.wait()


def place(whole, parts, starts, axis, shape):
    count = len(parts)
    continued = whole is not None
    vmem = pl.BlockSpec(memory_space=pltpu.VMEM)
    anywhere = pl.BlockSpec(memory_space=pl.ANY)
    return pl.pallas_call(
        lambda *refs: place_kernel(axis, count, *refs),
        out_shape=jax.ShapeDtypeStruct(shape, parts[0].dtype),
        in_specs=[pl.BlockSpec(memory_space=pltpu.SMEM)]
        + [vmem] * count
        + ([anywhere] if continued else []),
        out_specs=anywhere,
        scratch_shapes=[pltpu.SemaphoreType.DMA((count, 4))],
        input_output_aliases={1 + count: 0} if continued else {},
        name="place",
    )(jnp.stack(starts).astype(jnp.int32), *parts, *((whole,) if continued else ()))


def attend_kernel(scale, facts_ref, cosine_ref, sine_ref, new_ref, key_ref, value_ref, message_ref, query_s, message_s):
    groups, slots, _ = new_ref.shape
    rows, span, _ = key_ref.shape
    per_row = query_s.shape[0] // rows
    cosine, sine = cosine_ref[...], sine_ref[...]

    def turned(values):
        values = values.astype(jnp.float32)
        return values * cosine + pltpu.roll(values, HD // 2, 1) * sine

    for t in range(groups):
        for j in range(2):
            query = turned(new_ref[t, :, j * HD : (j + 1) * HD])
            for s in range(2):
                query_s[pl.ds(t * 4 + j * 2 + s, rows, stride=per_row), :] = query[
                    s * rows : (s + 1) * rows
                ]
    start, width = 2 * HD, KVH * HD // groups
    new_keys = jnp.concatenate([new_ref[t, :, start : start + width] for t in range(groups)], 1)
    new_keys = jnp.concatenate(
        [turned(new_keys[:, k * HD : (k + 1) * HD]) for k in range(KVH)], 1
    ).astype(jnp.bfloat16)
    new_values = jnp.concatenate(
        [new_ref[t, :, start + width : start + 2 * width] for t in range(groups)], 1
    )

    member = facts_ref[rows]
    kv_of = lax.broadcasted_iota(jnp.int32, (per_row, 1), 0) // (per_row // KVH)
    position = lax.broadcasted_iota(jnp.int32, (per_row, span), 1) + member * span
    slot = lax.broadcasted_iota(jnp.int32, (per_row, slots), 1)
    step = lax.broadcasted_iota(jnp.int32, (per_row, slots), 0) % 2
    lane = lax.broadcasted_iota(jnp.int32, (per_row, HD), 1)
    for r in range(rows):
        query = query_s[r * per_row : (r + 1) * per_row, :].astype(jnp.bfloat16)
        query = jnp.concatenate(
            [jnp.where(kv_of == k, query, jnp.zeros_like(query)) for k in range(KVH)], 1
        )

        def product(keys):
            return (
                lax.dot_general(
                    query, keys, (((1,), (1,)), ((), ())), preferred_element_type=jnp.float32
                )
                * scale
            )

        valid = position < facts_ref[r]
        scores = jnp.where(valid, product(key_ref[r]), FLOOR)
        fresh = (slot % rows == r) & (slot // rows <= step) & (member == 0)
        fresh_scores = jnp.where(fresh, product(new_keys), FLOOR)
        highest = jnp.maximum(
            jnp.max(scores, 1, keepdims=True), jnp.max(fresh_scores, 1, keepdims=True)
        )
        upper = highest.astype(jnp.bfloat16).astype(jnp.float32)
        lower = (highest - upper).astype(jnp.bfloat16).astype(jnp.float32)
        highest = upper + lower
        weights = jnp.where(valid, jnp.exp(scores - highest), 0.0)
        fresh_weights = jnp.where(fresh, jnp.exp(fresh_scores - highest), 0.0)
        total = jnp.sum(weights, 1, keepdims=True) + jnp.sum(fresh_weights, 1, keepdims=True)
        mixed = jnp.dot(
            weights.astype(jnp.bfloat16), value_ref[r], preferred_element_type=jnp.float32
        ) + jnp.dot(
            fresh_weights.astype(jnp.bfloat16), new_values, preferred_element_type=jnp.float32
        )
        own = jnp.zeros((per_row, HD), jnp.float32)
        for k in range(KVH):
            own = jnp.where(kv_of == k, mixed[:, k * HD : (k + 1) * HD], own)
        total_upper = total.astype(jnp.bfloat16).astype(jnp.float32)
        total_lower = total - total_upper
        facts = jnp.where(
            lane < 64,
            jnp.where(lane < 32, upper, lower),
            jnp.where(lane < 96, total_upper, total_lower),
        )
        for t in range(groups):
            message_s[t, pl.ds(r, 4, stride=rows), :] = own[t * 4 : (t + 1) * 4]
            message_s[t, pl.ds(4 * rows + r, 4, stride=rows), :] = facts[t * 4 : (t + 1) * 4]
    message_ref[...] = message_s[...].astype(message_ref.dtype)


def merge_kernel(message_ref, attended_ref):
    message = message_ref[...].astype(jnp.float32)
    half = message.shape[1] // 2
    facts = message[:, half:]
    highest = facts[:, :, 0:1] + facts[:, :, 32:33]
    totals = facts[:, :, 64:65] + facts[:, :, 96:97]
    rescale = jnp.exp(highest - jnp.max(highest, 0, keepdims=True))
    total = jnp.sum(totals * rescale, 0)
    mixture = jnp.sum(message[:, :half] * rescale, 0)
    attended = (mixture / total).astype(attended_ref.dtype)
    attended_ref[...] = jnp.concatenate([attended[: half // 2], attended[half // 2 :]], 1)


def project_kernel(attended_ref, weight_ref, terms_ref):
    terms = lax.dot_general(
        attended_ref[...],
        weight_ref[...],
        (((1,), (1,)), ((), ())),
        preferred_element_type=jnp.float32,
    )
    terms_ref[0] = terms.astype(terms_ref.dtype)


def exchange(blocks, axis):
    return lax.all_to_all(blocks, axis, split_axis=0, concat_axis=0, tiled=True)


def on_device(hidden, norm_gain, qkv_bias, key_cache, value_cache, lengths, fresh_qkv, fresh_out):
    groups = lax.axis_size("tensor")
    member = lax.axis_index("tensor")
    replicas = lax.axis_size("dp")
    step_count, row_count, feature_width = hidden.shape
    slots = step_count * row_count
    share = feature_width // replicas
    query_width = QH * HD // groups
    kv_width = KVH * HD // groups
    own_heads = QH // groups
    score_scale = 1.0 / math.sqrt(HD)

    replica = lax.axis_index("dp")
    column, y_at = replica // 4, replica % 4
    vmem = pl.BlockSpec(memory_space=pltpu.VMEM)
    smem = pl.BlockSpec(memory_space=pltpu.SMEM)
    anywhere = pl.BlockSpec(memory_space=pl.ANY)
    across = [(i, i ^ 4) for i in range(replicas)]
    ahead = [(i, (i & 4) | ((i + 1) & 3)) for i in range(replicas)]
    behind = [(i, (i & 4) | ((i + 3) & 3)) for i in range(replicas)]
    beyond = [(i, (i & 4) | ((i + 2) & 3)) for i in range(replicas)]

    def send(value, pairs):
        return lax.ppermute(value, "dp", pairs)

    width = 2 * query_width + HD
    group_width = query_width + 2 * kv_width
    packed, own_states, other_states = pl.pallas_call(
        lambda *refs: pack_kernel(groups, *refs),
        out_shape=(
            jax.ShapeDtypeStruct((groups, fresh_qkv.shape[0], width), fresh_qkv.dtype),
            jax.ShapeDtypeStruct((replicas // 2, slots, share), jnp.bfloat16),
            jax.ShapeDtypeStruct((replicas // 2, slots, share), jnp.bfloat16),
        ),
        in_specs=[smem] + [vmem] * 4,
        name="pack",
    )(
        jnp.stack([column, y_at]).astype(jnp.int32),
        hidden.reshape(slots, feature_width),
        norm_gain.reshape(1, feature_width),
        fresh_qkv,
        fresh_out,
    )
    packed = exchange(packed, "tensor").reshape(share, width)

    cross_states = send(other_states, across)
    low_states, far_states, high_states = (
        send(jnp.stack([own_states[k], cross_states[k]]), pairs)
        for k, pairs in ((1, ahead), (2, beyond), (3, behind))
    )
    order = jnp.stack(
        [(column ^ c) * 4 + ((y_at + y) & 3) for y in (0, -1, 1, 2) for c in (0, 1)]
    ).astype(jnp.int32)

    terms, own_out = pl.pallas_call(
        lambda *refs: terms_kernel(group_width, *refs),
        out_shape=(
            jax.ShapeDtypeStruct((replicas, slots, group_width), jnp.float32),
            jax.ShapeDtypeStruct((share, query_width), packed.dtype),
        ),
        in_specs=[smem] + [vmem] * 6,
        name="terms",
    )(order, own_states, cross_states, low_states, high_states, far_states, packed)
    terms = exchange(terms, "dp")
    out_across = send(own_out, across)
    out_low, out_high = send(own_out, ahead), send(own_out, behind)
    own_qkv = pl.pallas_call(
        turn_kernel,
        out_shape=jax.ShapeDtypeStruct((group_width, share), packed.dtype),
        name="turn",
    )(packed)
    moved = (out_across, out_low, out_high, own_qkv)
    projected, out_across, out_low, out_high, own_qkv = pl.pallas_call(
        lambda terms_ref, bias_ref, *refs: sum_kernel(groups, terms_ref, bias_ref, *refs),
        out_shape=(
            jax.ShapeDtypeStruct((groups, slots, group_width), jnp.bfloat16),
            *(jax.ShapeDtypeStruct(v.shape, v.dtype) for v in moved),
        ),
        in_specs=[vmem] * 2 + [anywhere] * 4,
        out_specs=(vmem,) + (anywhere,) * 4,
        input_output_aliases={2 + i: 1 + i for i in range(4)},
        name="sum",
    )(terms, qkv_bias.reshape(1, group_width), *moved)
    gathered = exchange(projected, "tensor")

    out_cross_low, out_cross_high = send(out_across, ahead), send(out_across, behind)
    qkv_low, qkv_high = send(own_qkv, ahead), send(own_qkv, behind)
    qkv_across = send(own_qkv, across)

    def index_of(column_at, y):
        return (column_at * 4 + ((y_at + y) & 3)) * (share // 512)

    other = 1 - column
    out_shape, qkv_shape = (feature_width, query_width), (group_width, feature_width)

    half_width = HD // 2
    inverse = THETA ** (-jnp.arange(half_width, dtype=jnp.float32) * 2.0 / HD)
    position = (lengths[None, :] + jnp.arange(step_count, dtype=jnp.int32)[:, None]).astype(
        jnp.float32
    )
    angles = position.reshape(slots, 1) * inverse
    cosine, sine = jnp.cos(angles), jnp.sin(angles)
    cosine = jnp.concatenate([cosine, cosine], 1)
    sine = jnp.concatenate([-sine, sine], 1)

    grouped_out = place(
        None, [own_out, out_across], [index_of(column, 0), index_of(other, 0)], 0, out_shape
    )
    grouped_out = place(
        grouped_out, [out_low, out_high], [index_of(column, -1), index_of(column, 1)], 0, out_shape
    )

    facts = jnp.concatenate([lengths, jnp.full((1,), member, jnp.int32)])
    message = pl.pallas_call(
        lambda *refs: attend_kernel(score_scale, *refs),
        out_shape=jax.ShapeDtypeStruct((groups, 2 * slots * own_heads, HD), jnp.bfloat16),
        in_specs=[smem] + [vmem] * 5,
        scratch_shapes=[
            pltpu.VMEM((slots * QH, HD), jnp.float32),
            pltpu.VMEM((groups, 2 * slots * own_heads, HD), jnp.float32),
        ],
        name="attend",
    )(facts, cosine, sine, gathered, key_cache, value_cache)
    message, out_cross_low, out_cross_high, qkv_low, qkv_high, qkv_across, grouped_out = hold(
        message, out_cross_low, out_cross_high, qkv_low, qkv_high, qkv_across, grouped_out
    )
    message = exchange(message, "tensor")
    out_far, out_cross_far = send(out_low, ahead), send(out_cross_high, behind)
    qkv_cross_high = send(qkv_high, across)
    grouped_out = place(
        grouped_out,
        [out_cross_low, out_cross_high],
        [index_of(other, -1), index_of(other, 1)],
        0,
        out_shape,
    )
    grouped_qkv = place(
        None, [own_qkv, qkv_across], [index_of(column, 0), index_of(other, 0)], 1, qkv_shape
    )
    attended = pl.pallas_call(
        merge_kernel,
        out_shape=jax.ShapeDtypeStruct((slots, own_heads * HD), jnp.bfloat16),
        name="merge",
    )(message)
    attended, out_far, out_cross_far, qkv_cross_high, qkv_low, grouped_out, grouped_qkv = hold(
        attended, out_far, out_cross_far, qkv_cross_high, qkv_low, grouped_out, grouped_qkv
    )
    grouped_out = place(
        grouped_out,
        [out_far, out_cross_far],
        [index_of(column, 2), index_of(other, 2)],
        0,
        out_shape,
    )
    qkv_far, qkv_cross_far = send(qkv_low, ahead), send(qkv_cross_high, behind)
    qkv_cross_low = send(qkv_low, across)
    grouped_qkv = place(
        grouped_qkv,
        [qkv_low, qkv_high, qkv_cross_high],
        [index_of(column, -1), index_of(column, 1), index_of(other, 1)],
        1,
        qkv_shape,
    )
    grouped_qkv = place(
        grouped_qkv,
        [qkv_far, qkv_cross_low, qkv_cross_far],
        [index_of(column, 2), index_of(other, -1), index_of(other, 2)],
        1,
        qkv_shape,
    ).T

    span = feature_width // groups
    term_sums = pl.pallas_call(
        project_kernel,
        grid=(groups,),
        out_shape=jax.ShapeDtypeStruct((groups, slots, span), jnp.bfloat16),
        in_specs=[
            pl.BlockSpec((slots, own_heads * HD), lambda i: (0, 0)),
            pl.BlockSpec((span, own_heads * HD), lambda i: (i, 0)),
        ],
        out_specs=pl.BlockSpec((1, slots, span), lambda i: (i, 0, 0)),
        name="project",
    )(attended, grouped_out)
    attn_output = jnp.sum(exchange(term_sums, "tensor").astype(jnp.float32), 0)
    attn_output = attn_output.astype(jnp.bfloat16).reshape(step_count, row_count, -1)
    return (attn_output, grouped_qkv, grouped_out)


def solution(mesh):
    return jax.shard_map(
        on_device,
        mesh=mesh,
        in_specs=(
            P(None, "dp", None),
            P(),
            P("tensor"),
            P("dp", "tensor", None),
            P("dp", "tensor", None),
            P("dp"),
            P(("dp", "tensor"), None),
            P(("dp", "tensor"), None),
        ),
        out_specs=(P(None, "dp", "tensor"), P(None, "tensor"), P(None, "tensor")),
        check_vma=False,
    )
```

```python
import math

import jax
import jax.numpy as jnp
from jax import lax
from jax.experimental import pallas as pl
from jax.experimental.pallas import tpu as pltpu
from jax.sharding import PartitionSpec as P

HD = 128
QH = 32
KVH = 4
THETA = 1000000.0
EPS = 1e-06
FLOOR = -1e30


def pack_kernel(groups, after_ref, qkv_ref, out_ref, packed_ref):
    query_width = QH * HD // groups
    kv_width = KVH * HD // groups
    rows = qkv_ref.shape[0]
    for g in range(groups):
        keys_at = QH * HD + g * kv_width
        values_at = QH * HD + KVH * HD + g * kv_width
        packed_ref[g, :, :query_width] = qkv_ref[:, g * query_width : (g + 1) * query_width]
        packed_ref[g, :, query_width : query_width + HD] = jnp.concatenate(
            [
                qkv_ref[:, keys_at : keys_at + kv_width],
                qkv_ref[:, values_at : values_at + kv_width],
                jnp.zeros((rows, HD - 2 * kv_width), qkv_ref.dtype),
            ],
            1,
        )
        packed_ref[g, :, query_width + HD :] = out_ref[:, g * query_width : (g + 1) * query_width]


def norm_kernel(states_ref, gain_ref, own_ref, send_ref):
    states = jnp.concatenate([states_ref[0], states_ref[1]], 0).astype(jnp.float32)
    normed = (
        states
        * lax.rsqrt(jnp.mean(states * states, -1, keepdims=True) + EPS)
        * gain_ref[...].astype(jnp.float32)
    ).astype(jnp.bfloat16)
    replica = lax.axis_index("dp")
    column, y_at = replica // 4, replica % 4
    count, _, share = own_ref.shape
    for y in range(count):
        first = normed[:, y * share : (y + 1) * share]
        second = normed[:, (count + y) * share : (count + y + 1) * share]
        slot = (y - y_at) & 3
        own_ref[slot] = jnp.where(column == 0, first, second)
        send_ref[slot] = jnp.where(column == 0, second, first)


def terms_kernel(group_width, own, got, low, high, far, packed_ref, terms_ref, out_ref):
    weights = packed_ref[:, :group_width]
    states = jnp.concatenate(
        [own[0], got[0], low[0], low[1], high[0], high[1], far[0], far[1]], 0
    )
    terms = jnp.dot(states, weights, preferred_element_type=jnp.float32)
    slots = own.shape[1]
    replica = lax.axis_index("dp")
    order = [(c, y) for y in (0, -1, 1, 2) for c in (0, 1)]
    for i, (c, y) in enumerate(order):
        source = ((replica // 4) ^ c) * 4 + ((replica + y) & 3)
        terms_ref[source] = terms[i * slots : (i + 1) * slots]
    out_ref[...] = packed_ref[:, group_width + 64 :]


def hold_kernel(*refs):
    pass


def hold(*values):
    anywhere = pl.BlockSpec(memory_space=pl.ANY)
    return pl.pallas_call(
        hold_kernel,
        out_shape=tuple(jax.ShapeDtypeStruct(v.shape, v.dtype) for v in values),
        in_specs=[anywhere] * len(values),
        out_specs=(anywhere,) * len(values),
        input_output_aliases={i: i for i in range(len(values))},
        name="hold",
    )(*values)


def sum_kernel(groups, terms_ref, bias_ref, *refs):
    projected_ref = refs[4]
    total = jnp.sum(terms_ref[...], 0) + bias_ref[...].astype(jnp.float32)
    total = total.astype(projected_ref.dtype)
    for g in range(groups):
        projected_ref[g] = total


def turn_kernel(packed_ref, turned_ref):
    width = turned_ref.shape[0]
    turned_ref[...] = packed_ref[:, : width + 64].T[:width]


def place_kernel(axis, where, *refs):
    parts, whole_ref, sems = refs[: len(where)], refs[-2], refs[-1]
    replica = lax.axis_index("dp")
    copies = []
    for i, (part, (c, y)) in enumerate(zip(parts, where)):
        size = part.shape[axis]
        source = ((replica // 4) ^ c) * 4 + ((replica + y) & 3)
        at = pl.ds(pl.multiple_of(source * size, size), size)
        target = whole_ref.at[at, :] if axis == 0 else whole_ref.at[:, at]
        copies.append(pltpu.make_async_copy(part, target, sems.at[i]))
    for copy in copies:
        copy.start()
    for copy in copies:
        copy.wait()


def place(whole, parts, where, axis, shape):
    count = len(parts)
    continued = whole is not None
    vmem = pl.BlockSpec(memory_space=pltpu.VMEM)
    anywhere = pl.BlockSpec(memory_space=pl.ANY)
    return pl.pallas_call(
        lambda *refs: place_kernel(axis, where, *refs),
        out_shape=jax.ShapeDtypeStruct(shape, parts[0].dtype),
        in_specs=[vmem] * count + ([anywhere] if continued else []),
        out_specs=anywhere,
        scratch_shapes=[pltpu.SemaphoreType.DMA((count,))],
        input_output_aliases={count: 0} if continued else {},
        name="place",
    )(*parts, *((whole,) if continued else ()))


def attend_kernel(scale, lengths_ref, cosine_ref, sine_ref, new_ref, key_ref, value_ref, message_ref, query_s, message_s):
    groups, slots, _ = new_ref.shape
    rows, span, _ = key_ref.shape
    per_row = query_s.shape[0] // rows
    cosine, sine = cosine_ref[...], sine_ref[...]

    def turned(values):
        values = values.astype(jnp.float32)
        return values * cosine + pltpu.roll(values, HD // 2, 1) * sine

    for t in range(groups):
        for j in range(2):
            query = turned(new_ref[t, :, j * HD : (j + 1) * HD])
            for s in range(2):
                query_s[pl.ds(t * 4 + j * 2 + s, rows, stride=per_row), :] = query[
                    s * rows : (s + 1) * rows
                ]
    start, width = 2 * HD, KVH * HD // groups
    new_keys = jnp.concatenate([new_ref[t, :, start : start + width] for t in range(groups)], 1)
    new_keys = jnp.concatenate(
        [turned(new_keys[:, k * HD : (k + 1) * HD]) for k in range(KVH)], 1
    ).astype(jnp.bfloat16)
    new_values = jnp.concatenate(
        [new_ref[t, :, start + width : start + 2 * width] for t in range(groups)], 1
    )

    member = lax.axis_index("tensor")
    kv_of = lax.broadcasted_iota(jnp.int32, (per_row, 1), 0) // (per_row // KVH)
    position = lax.broadcasted_iota(jnp.int32, (per_row, span), 1) + member * span
    slot = lax.broadcasted_iota(jnp.int32, (per_row, slots), 1)
    step = lax.broadcasted_iota(jnp.int32, (per_row, slots), 0) % 2
    lane = lax.broadcasted_iota(jnp.int32, (per_row, HD), 1)
    for r in range(rows):
        query = query_s[r * per_row : (r + 1) * per_row, :].astype(jnp.bfloat16)
        query = jnp.concatenate(
            [jnp.where(kv_of == k, query, jnp.zeros_like(query)) for k in range(KVH)], 1
        )

        def product(keys):
            return (
                lax.dot_general(
                    query, keys, (((1,), (1,)), ((), ())), preferred_element_type=jnp.float32
                )
                * scale
            )

        valid = position < lengths_ref[r]
        scores = jnp.where(valid, product(key_ref[r]), FLOOR)
        fresh = (slot % rows == r) & (slot // rows <= step) & (member == 0)
        fresh_scores = jnp.where(fresh, product(new_keys), FLOOR)
        highest = jnp.maximum(
            jnp.max(scores, 1, keepdims=True), jnp.max(fresh_scores, 1, keepdims=True)
        )
        upper = highest.astype(jnp.bfloat16).astype(jnp.float32)
        lower = (highest - upper).astype(jnp.bfloat16).astype(jnp.float32)
        highest = upper + lower
        weights = jnp.where(valid, jnp.exp(scores - highest), 0.0)
        fresh_weights = jnp.where(fresh, jnp.exp(fresh_scores - highest), 0.0)
        total = jnp.sum(weights, 1, keepdims=True) + jnp.sum(fresh_weights, 1, keepdims=True)
        mixed = jnp.dot(
            weights.astype(jnp.bfloat16), value_ref[r], preferred_element_type=jnp.float32
        ) + jnp.dot(
            fresh_weights.astype(jnp.bfloat16), new_values, preferred_element_type=jnp.float32
        )
        own = jnp.zeros((per_row, HD), jnp.float32)
        for k in range(KVH):
            own = jnp.where(kv_of == k, mixed[:, k * HD : (k + 1) * HD], own)
        total_upper = total.astype(jnp.bfloat16).astype(jnp.float32)
        total_lower = total - total_upper
        facts = jnp.where(
            lane < 64,
            jnp.where(lane < 32, upper, lower),
            jnp.where(lane < 96, total_upper, total_lower),
        )
        for t in range(groups):
            message_s[t, pl.ds(r, 4, stride=rows), :] = own[t * 4 : (t + 1) * 4]
            message_s[t, pl.ds(4 * rows + r, 4, stride=rows), :] = facts[t * 4 : (t + 1) * 4]
    message_ref[...] = message_s[...].astype(message_ref.dtype)


def merge_kernel(message_ref, attended_ref):
    message = message_ref[...].astype(jnp.float32)
    half = message.shape[1] // 2
    facts = message[:, half:]
    highest = facts[:, :, 0:1] + facts[:, :, 32:33]
    totals = facts[:, :, 64:65] + facts[:, :, 96:97]
    rescale = jnp.exp(highest - jnp.max(highest, 0, keepdims=True))
    total = jnp.sum(totals * rescale, 0)
    mixture = jnp.sum(message[:, :half] * rescale, 0)
    attended = (mixture / total).astype(attended_ref.dtype)
    attended_ref[...] = jnp.concatenate([attended[: half // 2], attended[half // 2 :]], 1)


def total_kernel(terms_ref, after_ref, output_ref):
    output_ref[...] = jnp.sum(terms_ref[...].astype(jnp.float32), 0).astype(output_ref.dtype)


def exchange(blocks, axis):
    return lax.all_to_all(blocks, axis, split_axis=0, concat_axis=0, tiled=True)


def on_device(hidden, norm_gain, qkv_bias, key_cache, value_cache, lengths, fresh_qkv, fresh_out):
    groups = lax.axis_size("tensor")
    replicas = lax.axis_size("dp")
    step_count, row_count, feature_width = hidden.shape
    slots = step_count * row_count
    share = feature_width // replicas
    query_width = QH * HD // groups
    kv_width = KVH * HD // groups
    own_heads = QH // groups
    score_scale = 1.0 / math.sqrt(HD)

    vmem = pl.BlockSpec(memory_space=pltpu.VMEM)
    smem = pl.BlockSpec(memory_space=pltpu.SMEM)
    anywhere = pl.BlockSpec(memory_space=pl.ANY)
    across = [(i, i ^ 4) for i in range(replicas)]
    ahead = [(i, (i & 4) | ((i + 1) & 3)) for i in range(replicas)]
    behind = [(i, (i & 4) | ((i + 3) & 3)) for i in range(replicas)]
    beyond = [(i, (i & 4) | ((i + 2) & 3)) for i in range(replicas)]

    def send(value, pairs):
        return lax.ppermute(value, "dp", pairs)

    width = 2 * query_width + HD
    group_width = query_width + 2 * kv_width
    own_states, other_states = pl.pallas_call(
        norm_kernel,
        out_shape=(jax.ShapeDtypeStruct((replicas // 2, slots, share), jnp.bfloat16),) * 2,
        name="norm",
    )(hidden, norm_gain.reshape(1, feature_width))
    cross_states = send(other_states, across)
    packed = pl.pallas_call(
        lambda *refs: pack_kernel(groups, *refs),
        out_shape=jax.ShapeDtypeStruct((groups, fresh_qkv.shape[0], width), fresh_qkv.dtype),
        in_specs=[anywhere] + [vmem] * 2,
        name="pack",
    )(own_states, fresh_qkv, fresh_out)
    packed, cross_states = hold(packed, cross_states)
    packed = exchange(packed, "tensor").reshape(share, width)

    low_states, far_states, high_states = (
        send(jnp.stack([own_states[k], cross_states[k]]), pairs)
        for k, pairs in ((1, ahead), (2, beyond), (3, behind))
    )
    terms, own_out = pl.pallas_call(
        lambda *refs: terms_kernel(group_width, *refs),
        out_shape=(
            jax.ShapeDtypeStruct((replicas, slots, group_width), jnp.float32),
            jax.ShapeDtypeStruct((share, query_width), packed.dtype),
        ),
        name="terms",
    )(own_states, cross_states, low_states, high_states, far_states, packed)
    terms = exchange(terms, "dp")
    out_across = send(own_out, across)
    out_low, out_high = send(own_out, ahead), send(own_out, behind)
    own_qkv = pl.pallas_call(
        turn_kernel,
        out_shape=jax.ShapeDtypeStruct((group_width, share), packed.dtype),
        name="turn",
    )(packed)
    moved = (out_across, out_low, out_high, own_qkv)
    projected, out_across, out_low, out_high, own_qkv = pl.pallas_call(
        lambda terms_ref, bias_ref, *refs: sum_kernel(groups, terms_ref, bias_ref, *refs),
        out_shape=(
            jax.ShapeDtypeStruct((groups, slots, group_width), jnp.bfloat16),
            *(jax.ShapeDtypeStruct(v.shape, v.dtype) for v in moved),
        ),
        in_specs=[vmem] * 2 + [anywhere] * 4,
        out_specs=(vmem,) + (anywhere,) * 4,
        input_output_aliases={2 + i: 1 + i for i in range(4)},
        name="sum",
    )(terms, qkv_bias.reshape(1, group_width), *moved)
    gathered = exchange(projected, "tensor")

    out_cross_low, out_cross_high = send(out_across, ahead), send(out_across, behind)
    qkv_low, qkv_high = send(own_qkv, ahead), send(own_qkv, behind)
    qkv_across = send(own_qkv, across)

    out_shape, qkv_shape = (feature_width, query_width), (group_width, feature_width)

    half_width = HD // 2
    inverse = THETA ** (-jnp.arange(half_width, dtype=jnp.float32) * 2.0 / HD)
    position = (lengths[None, :] + jnp.arange(step_count, dtype=jnp.int32)[:, None]).astype(
        jnp.float32
    )
    angles = position.reshape(slots, 1) * inverse
    cosine, sine = jnp.cos(angles), jnp.sin(angles)
    cosine = jnp.concatenate([cosine, cosine], 1)
    sine = jnp.concatenate([-sine, sine], 1)

    grouped_out = place(
        None, [own_out, out_across], [(0, 0), (1, 0)], 0, out_shape
    )
    grouped_out = place(
        grouped_out, [out_low, out_high], [(0, -1), (0, 1)], 0, out_shape
    )

    message = pl.pallas_call(
        lambda *refs: attend_kernel(score_scale, *refs),
        out_shape=jax.ShapeDtypeStruct((groups, 2 * slots * own_heads, HD), jnp.bfloat16),
        in_specs=[smem] + [vmem] * 5,
        scratch_shapes=[
            pltpu.VMEM((slots * QH, HD), jnp.float32),
            pltpu.VMEM((groups, 2 * slots * own_heads, HD), jnp.float32),
        ],
        name="attend",
    )(lengths, cosine, sine, gathered, key_cache, value_cache)
    message, out_cross_low, out_cross_high, qkv_low, qkv_high, qkv_across, grouped_out = hold(
        message, out_cross_low, out_cross_high, qkv_low, qkv_high, qkv_across, grouped_out
    )
    message = exchange(message, "tensor")
    out_far, out_cross_far = send(out_low, ahead), send(out_cross_high, behind)
    qkv_cross_high = send(qkv_high, across)
    grouped_out = place(
        grouped_out,
        [out_cross_low, out_cross_high],
        [(1, -1), (1, 1)],
        0,
        out_shape,
    )
    grouped_qkv = place(
        None, [own_qkv, qkv_across], [(0, 0), (1, 0)], 1, qkv_shape
    )
    attended = pl.pallas_call(
        merge_kernel,
        out_shape=jax.ShapeDtypeStruct((slots, own_heads * HD), jnp.bfloat16),
        name="merge",
    )(message)
    attended, out_far, out_cross_far, qkv_cross_high, qkv_low, grouped_out, grouped_qkv = hold(
        attended, out_far, out_cross_far, qkv_cross_high, qkv_low, grouped_out, grouped_qkv
    )
    grouped_out = place(
        grouped_out,
        [out_far, out_cross_far],
        [(0, 2), (1, 2)],
        0,
        out_shape,
    )
    qkv_far, qkv_cross_far = send(qkv_low, ahead), send(qkv_cross_high, behind)
    qkv_cross_low = send(qkv_low, across)
    grouped_qkv = place(
        grouped_qkv,
        [qkv_low, qkv_high, qkv_cross_high],
        [(0, -1), (0, 1), (1, 1)],
        1,
        qkv_shape,
    )
    grouped_qkv = place(
        grouped_qkv,
        [qkv_far, qkv_cross_low, qkv_cross_far],
        [(0, 2), (1, -1), (1, 2)],
        1,
        qkv_shape,
    )

    term_sums = jnp.dot(attended, grouped_out.T, preferred_element_type=jnp.float32)
    term_sums = term_sums.astype(jnp.bfloat16).reshape(slots, groups, -1).transpose(1, 0, 2)
    term_sums = exchange(term_sums, "tensor")
    attn_output = pl.pallas_call(
        total_kernel,
        out_shape=jax.ShapeDtypeStruct((slots, feature_width // groups), jnp.bfloat16),
        in_specs=[vmem, anywhere],
        name="total",
    )(term_sums, grouped_qkv)
    attn_output = attn_output.reshape(step_count, row_count, -1)
    return (attn_output, grouped_qkv.T, grouped_out)


def solution(mesh):
    return jax.shard_map(
        on_device,
        mesh=mesh,
        in_specs=(
            P(None, "dp", None),
            P(),
            P("tensor"),
            P("dp", "tensor", None),
            P("dp", "tensor", None),
            P("dp"),
            P(("dp", "tensor"), None),
            P(("dp", "tensor"), None),
        ),
        out_specs=(P(None, "dp", "tensor"), P(None, "tensor"), P(None, "tensor")),
        check_vma=False,
    )
```

```python
import math

import jax
import jax.numpy as jnp
from jax import lax
from jax.experimental import pallas as pl
from jax.experimental.pallas import tpu as pltpu
from jax.sharding import PartitionSpec as P

HD = 128
QH = 32
KVH = 4
THETA = 1000000.0
EPS = 1e-06
FLOOR = -1e30


def pack_kernel(groups, after_ref, qkv_ref, out_ref, packed_ref):
    query_width = QH * HD // groups
    kv_width = KVH * HD // groups
    rows = qkv_ref.shape[0]
    quarter = rows // 4
    for g in range(groups):
        keys_at = QH * HD + g * kv_width
        values_at = QH * HD + KVH * HD + g * kv_width
        at = slice(g * query_width, (g + 1) * query_width)
        packed_ref[g, :rows, :] = qkv_ref[:, at]
        packed_ref[g, rows : 2 * rows, :] = out_ref[:, at]
        pair = jnp.concatenate(
            [
                qkv_ref[:, keys_at : keys_at + kv_width],
                qkv_ref[:, values_at : values_at + kv_width],
            ],
            1,
        )
        packed_ref[g, 2 * rows :, :] = jnp.concatenate(
            [pair[i * quarter : (i + 1) * quarter] for i in range(4)], 1
        )


def unpacked(packed_ref):
    groups, rows, query_width = packed_ref.shape
    rows = rows * 4 // 9
    pair_width = query_width // 4
    queries = jnp.concatenate([packed_ref[t, :rows, :] for t in range(groups)], 0)
    pairs = jnp.concatenate(
        [
            packed_ref[t, 2 * rows :, i * pair_width : (i + 1) * pair_width]
            for t in range(groups)
            for i in range(4)
        ],
        0,
    )
    return queries, pairs


def norm_kernel(states_ref, gain_ref, own_ref, send_ref):
    states = jnp.concatenate([states_ref[0], states_ref[1]], 0).astype(jnp.float32)
    normed = (
        states
        * lax.rsqrt(jnp.mean(states * states, -1, keepdims=True) + EPS)
        * gain_ref[...].reshape(1, -1).astype(jnp.float32)
    ).astype(jnp.bfloat16)
    replica = lax.axis_index("dp")
    column, y_at = replica // 4, replica % 4
    count, _, share = own_ref.shape
    for y in range(count):
        first = normed[:, y * share : (y + 1) * share]
        second = normed[:, (count + y) * share : (count + y + 1) * share]
        slot = (y - y_at) & 3
        own_ref[slot] = jnp.where(column == 0, first, second)
        send_ref[slot] = jnp.where(column == 0, second, first)


def terms_kernel(own, got, low, high, far, packed_ref, terms_ref, out_ref):
    states = jnp.concatenate(
        [own[0], got[0], low[0], low[1], high[0], high[1], far[0], far[1]], 0
    )
    terms = jnp.concatenate(
        [
            jnp.dot(states, weights, preferred_element_type=jnp.float32)
            for weights in unpacked(packed_ref)
        ],
        1,
    ).astype(terms_ref.dtype)
    slots = own.shape[1]
    replica = lax.axis_index("dp")
    order = [(c, y) for y in (0, -1, 1, 2) for c in (0, 1)]
    for i, (c, y) in enumerate(order):
        source = ((replica // 4) ^ c) * 4 + ((replica + y) & 3)
        terms_ref[source] = terms[i * slots : (i + 1) * slots]
    groups, rows, _ = packed_ref.shape
    rows = rows * 4 // 9
    for t in range(groups):
        out_ref[t * rows : (t + 1) * rows] = packed_ref[t, rows : 2 * rows, :]


def hold_kernel(*refs):
    pass


def hold(*values):
    anywhere = pl.BlockSpec(memory_space=pl.ANY)
    return pl.pallas_call(
        hold_kernel,
        out_shape=tuple(jax.ShapeDtypeStruct(v.shape, v.dtype) for v in values),
        in_specs=[anywhere] * len(values),
        out_specs=(anywhere,) * len(values),
        input_output_aliases={i: i for i in range(len(values))},
        compiler_params=pltpu.CompilerParams(vmem_limit_bytes=1 << 20),
        name="hold",
    )(*values)


def sum_kernel(groups, terms_ref, bias_ref, projected_ref):
    total = jnp.sum(terms_ref[...].astype(jnp.float32), 0) + bias_ref[...].astype(jnp.float32)
    total = total.astype(projected_ref.dtype)
    for g in range(groups):
        projected_ref[g] = total


def turn_kernel(packed_ref, turned_ref):
    queries, pairs = unpacked(packed_ref)
    width = queries.shape[1]
    turned_ref[:width] = queries.T
    turned_ref[width:] = pairs.T


def place_kernel(axis, where, *refs):
    parts = refs[: len(where)]
    replica = lax.axis_index("dp")
    whole_ref, sems = refs[-2:]
    copies = []
    for i, (part, (c, y)) in enumerate(zip(parts, where)):
        size = part.shape[axis]
        source = ((replica // 4) ^ c) * 4 + ((replica + y) & 3)
        at = pl.ds(pl.multiple_of(source * size, size), size)
        target = whole_ref.at[at, :] if axis == 0 else whole_ref.at[:, at]
        copies.append(pltpu.make_async_copy(part, target, sems.at[i]))
    for copy in copies:
        copy.start()
    for copy in copies:
        copy.wait()


def place(whole, parts, where, axis, shape):
    count = len(parts)
    continued = whole is not None
    vmem = pl.BlockSpec(memory_space=pltpu.VMEM)
    anywhere = pl.BlockSpec(memory_space=pl.ANY)
    return pl.pallas_call(
        lambda *refs: place_kernel(axis, where, *refs),
        out_shape=jax.ShapeDtypeStruct(shape, parts[0].dtype),
        in_specs=[vmem] * count + ([anywhere] if continued else []),
        out_specs=anywhere,
        scratch_shapes=[pltpu.SemaphoreType.DMA((count,))],
        input_output_aliases={count: 0} if continued else {},
        compiler_params=pltpu.CompilerParams(vmem_limit_bytes=4 << 20),
        name="place",
    )(*parts, *((whole,) if continued else ()))


def attend_kernel(scale, lengths_ref, cosine_ref, sine_ref, new_ref, key_ref, value_ref, message_ref, query_s, message_s):
    groups, slots, _ = new_ref.shape
    rows, span, _ = key_ref.shape
    per_row = query_s.shape[0] // rows
    cosine, sine = cosine_ref[...], sine_ref[...]

    def turned(values):
        values = values.astype(jnp.float32)
        return values * cosine + pltpu.roll(values, HD // 2, 1) * sine

    for t in range(groups):
        for j in range(2):
            query = turned(new_ref[t, :, j * HD : (j + 1) * HD])
            for s in range(2):
                query_s[pl.ds(t * 4 + j * 2 + s, rows, stride=per_row), :] = query[
                    s * rows : (s + 1) * rows
                ]
    start, width = 2 * HD, KVH * HD // groups
    new_keys = jnp.concatenate([new_ref[t, :, start : start + width] for t in range(groups)], 1)
    new_keys = jnp.concatenate(
        [turned(new_keys[:, k * HD : (k + 1) * HD]) for k in range(KVH)], 1
    ).astype(jnp.bfloat16)
    new_values = jnp.concatenate(
        [new_ref[t, :, start + width : start + 2 * width] for t in range(groups)], 1
    )

    member = lax.axis_index("tensor")
    kv_of = lax.broadcasted_iota(jnp.int32, (per_row, 1), 0) // (per_row // KVH)
    position = lax.broadcasted_iota(jnp.int32, (per_row, span), 1) + member * span
    slot = lax.broadcasted_iota(jnp.int32, (per_row, slots), 1)
    step = lax.broadcasted_iota(jnp.int32, (per_row, slots), 0) % 2
    lane = lax.broadcasted_iota(jnp.int32, (per_row, HD), 1)
    for r in range(rows):
        query = query_s[r * per_row : (r + 1) * per_row, :].astype(jnp.bfloat16)
        query = jnp.concatenate(
            [jnp.where(kv_of == k, query, jnp.zeros_like(query)) for k in range(KVH)], 1
        )

        def product(keys):
            return (
                lax.dot_general(
                    query, keys, (((1,), (1,)), ((), ())), preferred_element_type=jnp.float32
                )
                * scale
            )

        valid = position < lengths_ref[r]
        scores = jnp.where(valid, product(key_ref[r]), FLOOR)
        fresh = (slot % rows == r) & (slot // rows <= step) & (member == 0)
        fresh_scores = jnp.where(fresh, product(new_keys), FLOOR)
        highest = jnp.maximum(
            jnp.max(scores, 1, keepdims=True), jnp.max(fresh_scores, 1, keepdims=True)
        )
        upper = highest.astype(jnp.bfloat16).astype(jnp.float32)
        lower = (highest - upper).astype(jnp.bfloat16).astype(jnp.float32)
        highest = upper + lower
        weights = jnp.where(valid, jnp.exp(scores - highest), 0.0)
        fresh_weights = jnp.where(fresh, jnp.exp(fresh_scores - highest), 0.0)
        total = jnp.sum(weights, 1, keepdims=True) + jnp.sum(fresh_weights, 1, keepdims=True)
        mixed = jnp.dot(
            weights.astype(jnp.bfloat16), value_ref[r], preferred_element_type=jnp.float32
        ) + jnp.dot(
            fresh_weights.astype(jnp.bfloat16), new_values, preferred_element_type=jnp.float32
        )
        own = jnp.zeros((per_row, HD), jnp.float32)
        for k in range(KVH):
            own = jnp.where(kv_of == k, mixed[:, k * HD : (k + 1) * HD], own)
        total_upper = total.astype(jnp.bfloat16).astype(jnp.float32)
        total_lower = total - total_upper
        part = lane // 16 % 4
        facts = jnp.where(
            part < 2,
            jnp.where(part == 0, upper, lower),
            jnp.where(part == 2, total_upper, total_lower),
        )
        facts = jnp.where(lane < 64, facts, pltpu.roll(facts, per_row - 2, 0))
        for t in range(groups):
            message_s[t, pl.ds(r, 4, stride=rows), :] = own[t * 4 : (t + 1) * 4]
            message_s[t, pl.ds(4 * rows + r, 2, stride=rows), :] = facts[t * 4 : t * 4 + 2]
    message_ref[...] = message_s[...].astype(message_ref.dtype)


def merge_kernel(message_ref, attended_ref):
    message = message_ref[...].astype(jnp.float32)
    half = message.shape[1] * 2 // 3
    facts = message[:, half:]

    def fact(i):
        at = (16 * i, 64 + 16 * i)
        return jnp.concatenate([facts[:, :, lane : lane + 1] for lane in at], 1)

    highest, totals = fact(0) + fact(1), fact(2) + fact(3)
    rescale = jnp.exp(highest - jnp.max(highest, 0, keepdims=True))
    total = jnp.sum(totals * rescale, 0)
    mixture = jnp.sum(message[:, :half] * rescale, 0)
    attended = (mixture / total).astype(attended_ref.dtype)
    attended_ref[...] = jnp.concatenate([attended[: half // 2], attended[half // 2 :]], 1)


def total_kernel(terms_ref, after_ref, output_ref):
    output_ref[...] = jnp.sum(terms_ref[...].astype(jnp.float32), 0).astype(output_ref.dtype)


def exchange(blocks, axis):
    return lax.all_to_all(blocks, axis, split_axis=0, concat_axis=0, tiled=True)


def on_device(hidden, norm_gain, qkv_bias, key_cache, value_cache, lengths, fresh_qkv, fresh_out):
    groups = lax.axis_size("tensor")
    replicas = lax.axis_size("dp")
    step_count, row_count, feature_width = hidden.shape
    slots = step_count * row_count
    share = feature_width // replicas
    query_width = QH * HD // groups
    kv_width = KVH * HD // groups
    own_heads = QH // groups
    score_scale = 1.0 / math.sqrt(HD)

    vmem = pl.BlockSpec(memory_space=pltpu.VMEM)
    smem = pl.BlockSpec(memory_space=pltpu.SMEM)
    anywhere = pl.BlockSpec(memory_space=pl.ANY)
    across = [(i, i ^ 4) for i in range(replicas)]
    ahead = [(i, (i & 4) | ((i + 1) & 3)) for i in range(replicas)]
    behind = [(i, (i & 4) | ((i + 3) & 3)) for i in range(replicas)]
    beyond = [(i, (i & 4) | ((i + 2) & 3)) for i in range(replicas)]

    def send(value, pairs):
        return lax.ppermute(value, "dp", pairs)

    group_width = query_width + 2 * kv_width
    own_states, other_states = pl.pallas_call(
        norm_kernel,
        out_shape=(jax.ShapeDtypeStruct((replicas // 2, slots, share), jnp.bfloat16),) * 2,
        compiler_params=pltpu.CompilerParams(vmem_limit_bytes=6 << 20),
        name="norm",
    )(hidden, norm_gain)
    cross_states = send(other_states, across)
    packed = pl.pallas_call(
        lambda *refs: pack_kernel(groups, *refs),
        out_shape=jax.ShapeDtypeStruct((groups, fresh_qkv.shape[0] * 9 // 4, query_width), fresh_qkv.dtype),
        in_specs=[anywhere] + [vmem] * 2,
        compiler_params=pltpu.CompilerParams(vmem_limit_bytes=6 << 20),
        name="pack",
    )(own_states, fresh_qkv, fresh_out)
    packed, cross_states = hold(packed, cross_states)
    packed = exchange(packed, "tensor")

    low_states, far_states, high_states = (
        send(jnp.stack([own_states[k], cross_states[k]]), pairs)
        for k, pairs in ((1, ahead), (2, beyond), (3, behind))
    )
    terms, own_out = pl.pallas_call(
        terms_kernel,
        out_shape=(
            jax.ShapeDtypeStruct((replicas, slots, group_width), jnp.bfloat16),
            jax.ShapeDtypeStruct((share, query_width), packed.dtype),
        ),
        compiler_params=pltpu.CompilerParams(vmem_limit_bytes=8 << 20),
        name="terms",
    )(own_states, cross_states, low_states, high_states, far_states, packed)
    terms = exchange(terms, "dp")
    out_across = send(own_out, across)
    out_low, out_high = send(own_out, ahead), send(own_out, behind)
    own_qkv = pl.pallas_call(
        turn_kernel,
        out_shape=jax.ShapeDtypeStruct((group_width, share), packed.dtype),
        compiler_params=pltpu.CompilerParams(vmem_limit_bytes=4 << 20),
        name="turn",
    )(packed)
    moved = (out_across, own_qkv)
    projected, out_across, own_qkv = pl.pallas_call(
        lambda terms_ref, bias_ref, *refs: sum_kernel(groups, terms_ref, bias_ref, refs[4]),
        out_shape=(
            jax.ShapeDtypeStruct((groups, slots, group_width), jnp.bfloat16),
            *(jax.ShapeDtypeStruct(v.shape, v.dtype) for v in moved),
        ),
        in_specs=[vmem] * 2 + [anywhere] * 4,
        out_specs=(vmem,) + (anywhere,) * 2,
        input_output_aliases={2: 1, 3: 2},
        compiler_params=pltpu.CompilerParams(vmem_limit_bytes=3 << 20),
        name="sum",
    )(terms, qkv_bias.reshape(1, group_width), *moved, out_low, out_high)
    gathered = exchange(projected, "tensor")

    out_cross_low, out_cross_high = send(out_across, ahead), send(out_across, behind)
    qkv_low, qkv_high = send(own_qkv, ahead), send(own_qkv, behind)
    qkv_across = send(own_qkv, across)

    out_shape, qkv_shape = (feature_width, query_width), (group_width, feature_width)

    half_width = HD // 2
    inverse = THETA ** (-jnp.arange(half_width, dtype=jnp.float32) * 2.0 / HD)
    position = (lengths[None, :] + jnp.arange(step_count, dtype=jnp.int32)[:, None]).astype(
        jnp.float32
    )
    angles = position.reshape(slots, 1) * inverse
    cosine, sine = jnp.cos(angles), jnp.sin(angles)
    cosine = jnp.concatenate([cosine, cosine], 1)
    sine = jnp.concatenate([-sine, sine], 1)

    grouped_out = place(
        None, [own_out, out_across], [(0, 0), (1, 0)], 0, out_shape
    )
    grouped_out = place(
        grouped_out, [out_low, out_high], [(0, -1), (0, 1)], 0, out_shape
    )

    message = pl.pallas_call(
        lambda *refs: attend_kernel(score_scale, *refs),
        out_shape=jax.ShapeDtypeStruct((groups, 3 * slots, HD), jnp.bfloat16),
        in_specs=[smem] + [vmem] * 5,
        scratch_shapes=[
            pltpu.VMEM((slots * QH, HD), jnp.float32),
            pltpu.VMEM((groups, 3 * slots, HD), jnp.float32),
        ],
        compiler_params=pltpu.CompilerParams(vmem_limit_bytes=14 << 20),
        name="attend",
    )(lengths, cosine, sine, gathered, key_cache, value_cache)
    message, out_cross_low, out_cross_high, qkv_low, qkv_high, qkv_across, grouped_out = hold(
        message, out_cross_low, out_cross_high, qkv_low, qkv_high, qkv_across, grouped_out
    )
    message = exchange(message, "tensor")
    out_far, out_cross_far = send(out_low, ahead), send(out_cross_high, behind)
    qkv_cross_high = send(qkv_high, across)
    grouped_out = place(
        grouped_out,
        [out_cross_low, out_cross_high],
        [(1, -1), (1, 1)],
        0,
        out_shape,
    )
    grouped_qkv = place(
        None, [own_qkv, qkv_across], [(0, 0), (1, 0)], 1, qkv_shape
    )
    attended = pl.pallas_call(
        merge_kernel,
        out_shape=jax.ShapeDtypeStruct((slots, own_heads * HD), jnp.bfloat16),
        compiler_params=pltpu.CompilerParams(vmem_limit_bytes=3 << 20),
        name="merge",
    )(message)
    attended, out_far, out_cross_far, qkv_cross_high, qkv_low, grouped_out, grouped_qkv = hold(
        attended, out_far, out_cross_far, qkv_cross_high, qkv_low, grouped_out, grouped_qkv
    )
    grouped_out = place(
        grouped_out,
        [out_far, out_cross_far],
        [(0, 2), (1, 2)],
        0,
        out_shape,
    )
    qkv_far, qkv_cross_far = send(qkv_low, ahead), send(qkv_cross_high, behind)
    qkv_cross_low = send(qkv_low, across)
    grouped_qkv = place(
        grouped_qkv,
        [qkv_low, qkv_high, qkv_cross_high],
        [(0, -1), (0, 1), (1, 1)],
        1,
        qkv_shape,
    )
    grouped_qkv = place(
        grouped_qkv,
        [qkv_far, qkv_cross_low, qkv_cross_far],
        [(0, 2), (1, -1), (1, 2)],
        1,
        qkv_shape,
    )

    term_sums = jnp.dot(attended, grouped_out.T, preferred_element_type=jnp.float32)
    term_sums = term_sums.astype(jnp.bfloat16).reshape(slots, groups, -1).transpose(1, 0, 2)
    term_sums = exchange(term_sums, "tensor")
    attn_output = pl.pallas_call(
        total_kernel,
        out_shape=jax.ShapeDtypeStruct((slots, feature_width // groups), jnp.bfloat16),
        in_specs=[vmem, anywhere],
        compiler_params=pltpu.CompilerParams(vmem_limit_bytes=56 << 20),
        name="total",
    )(term_sums, grouped_qkv)
    attn_output = attn_output.reshape(step_count, row_count, -1)
    return (attn_output, grouped_qkv.T, grouped_out)


def solution(mesh):
    return jax.shard_map(
        on_device,
        mesh=mesh,
        in_specs=(
            P(None, "dp", None),
            P(),
            P("tensor"),
            P("dp", "tensor", None),
            P("dp", "tensor", None),
            P("dp"),
            P(("dp", "tensor"), None),
            P(("dp", "tensor"), None),
        ),
        out_specs=(P(None, "dp", "tensor"), P(None, "tensor"), P(None, "tensor")),
        check_vma=False,
    )
```

```python
import math

import jax
import jax.numpy as jnp
from jax import lax
from jax.experimental import pallas as pl
from jax.experimental.pallas import tpu as pltpu
from jax.sharding import PartitionSpec as P

HD = 128
QH = 32
KVH = 4
THETA = 1000000.0
EPS = 1e-06
FLOOR = -1e30


def pack_kernel(groups, after_ref, qkv_ref, out_ref, packed_ref):
    query_width = QH * HD // groups
    kv_width = KVH * HD // groups
    rows = qkv_ref.shape[0]
    quarter = rows // 4
    for g in range(groups):
        keys_at = QH * HD + g * kv_width
        values_at = QH * HD + KVH * HD + g * kv_width
        at = slice(g * query_width, (g + 1) * query_width)
        packed_ref[g, :rows, :] = qkv_ref[:, at]
        packed_ref[g, rows : 2 * rows, :] = out_ref[:, at]
        pair = jnp.concatenate(
            [
                qkv_ref[:, keys_at : keys_at + kv_width],
                qkv_ref[:, values_at : values_at + kv_width],
            ],
            1,
        )
        packed_ref[g, 2 * rows :, :] = jnp.concatenate(
            [pair[i * quarter : (i + 1) * quarter] for i in range(4)], 1
        )


def unpacked(packed_ref):
    groups, rows, query_width = packed_ref.shape
    rows = rows * 4 // 9
    pair_width = query_width // 4
    queries = jnp.concatenate([packed_ref[t, :rows, :] for t in range(groups)], 0)
    pairs = jnp.concatenate(
        [
            packed_ref[t, 2 * rows :, i * pair_width : (i + 1) * pair_width]
            for t in range(groups)
            for i in range(4)
        ],
        0,
    )
    return queries, pairs


def norm_kernel(states_ref, gain_ref, own_ref, send_ref):
    states = jnp.concatenate([states_ref[0], states_ref[1]], 0).astype(jnp.float32)
    normed = (
        states
        * lax.rsqrt(jnp.mean(states * states, -1, keepdims=True) + EPS)
        * gain_ref[...].reshape(1, -1).astype(jnp.float32)
    ).astype(jnp.bfloat16)
    replica = lax.axis_index("dp")
    column, y_at = replica // 4, replica % 4
    count, _, share = own_ref.shape
    for y in range(count):
        first = normed[:, y * share : (y + 1) * share]
        second = normed[:, (count + y) * share : (count + y + 1) * share]
        slot = (y - y_at) & 3
        own_ref[slot] = jnp.where(column == 0, first, second)
        send_ref[slot] = jnp.where(column == 0, second, first)


def terms_kernel(own, got, low, high, far, packed_ref, terms_ref, out_ref):
    states = jnp.concatenate(
        [own[0], got[0], low[0], low[1], high[0], high[1], far[0], far[1]], 0
    )
    terms = jnp.concatenate(
        [
            jnp.dot(states, weights, preferred_element_type=jnp.float32)
            for weights in unpacked(packed_ref)
        ],
        1,
    ).astype(terms_ref.dtype)
    slots = own.shape[1]
    replica = lax.axis_index("dp")
    order = [(c, y) for y in (0, -1, 1, 2) for c in (0, 1)]
    for i, (c, y) in enumerate(order):
        source = ((replica // 4) ^ c) * 4 + ((replica + y) & 3)
        terms_ref[source] = terms[i * slots : (i + 1) * slots]
    groups, rows, _ = packed_ref.shape
    rows = rows * 4 // 9
    for t in range(groups):
        out_ref[t * rows : (t + 1) * rows] = packed_ref[t, rows : 2 * rows, :]


def hold_kernel(*refs):
    pass


def hold(*values):
    anywhere = pl.BlockSpec(memory_space=pl.ANY)
    return pl.pallas_call(
        hold_kernel,
        out_shape=tuple(jax.ShapeDtypeStruct(v.shape, v.dtype) for v in values),
        in_specs=[anywhere] * len(values),
        out_specs=(anywhere,) * len(values),
        input_output_aliases={i: i for i in range(len(values))},
        compiler_params=pltpu.CompilerParams(vmem_limit_bytes=1 << 20),
        name="hold",
    )(*values)


def sum_kernel(groups, terms_ref, bias_ref, projected_ref):
    total = jnp.sum(terms_ref[...].astype(jnp.float32), 0) + bias_ref[...].astype(jnp.float32)
    total = total.astype(projected_ref.dtype)
    for g in range(groups):
        projected_ref[g] = total


def turn_kernel(packed_ref, turned_ref):
    queries, pairs = unpacked(packed_ref)
    width = queries.shape[1]
    turned_ref[:width] = queries.T
    turned_ref[width:] = pairs.T


def place_kernel(axis, where, *refs):
    parts = refs[: len(where)]
    replica = lax.axis_index("dp")
    whole_ref, sems = refs[-2:]
    copies = []
    for i, (part, (c, y)) in enumerate(zip(parts, where)):
        size = part.shape[axis]
        source = ((replica // 4) ^ c) * 4 + ((replica + y) & 3)
        at = pl.ds(pl.multiple_of(source * size, size), size)
        target = whole_ref.at[at, :] if axis == 0 else whole_ref.at[:, at]
        copies.append(pltpu.make_async_copy(part, target, sems.at[i]))
    for copy in copies:
        copy.start()
    for copy in copies:
        copy.wait()


def place(whole, parts, where, axis, shape):
    count = len(parts)
    continued = whole is not None
    vmem = pl.BlockSpec(memory_space=pltpu.VMEM)
    anywhere = pl.BlockSpec(memory_space=pl.ANY)
    return pl.pallas_call(
        lambda *refs: place_kernel(axis, where, *refs),
        out_shape=jax.ShapeDtypeStruct(shape, parts[0].dtype),
        in_specs=[vmem] * count + ([anywhere] if continued else []),
        out_specs=anywhere,
        scratch_shapes=[pltpu.SemaphoreType.DMA((count,))],
        input_output_aliases={count: 0} if continued else {},
        compiler_params=pltpu.CompilerParams(vmem_limit_bytes=4 << 20),
        name="place",
    )(*parts, *((whole,) if continued else ()))


def attend_kernel(scale, lengths_ref, cosine_ref, sine_ref, new_ref, key_ref, value_ref, message_ref, query_s, message_s):
    groups, slots, _ = new_ref.shape
    rows, span, _ = key_ref.shape
    per_row = query_s.shape[0] // rows
    cosine, sine = cosine_ref[...], sine_ref[...]

    def turned(values):
        values = values.astype(jnp.float32)
        return values * cosine + pltpu.roll(values, HD // 2, 1) * sine

    for t in range(groups):
        for j in range(2):
            query = turned(new_ref[t, :, j * HD : (j + 1) * HD])
            for s in range(2):
                query_s[pl.ds(t * 4 + j * 2 + s, rows, stride=per_row), :] = query[
                    s * rows : (s + 1) * rows
                ]
    start, width = 2 * HD, KVH * HD // groups
    new_keys = jnp.concatenate([new_ref[t, :, start : start + width] for t in range(groups)], 1)
    new_keys = jnp.concatenate(
        [turned(new_keys[:, k * HD : (k + 1) * HD]) for k in range(KVH)], 1
    ).astype(jnp.bfloat16)
    new_values = jnp.concatenate(
        [new_ref[t, :, start + width : start + 2 * width] for t in range(groups)], 1
    )

    member = lax.axis_index("tensor")
    kv_of = lax.broadcasted_iota(jnp.int32, (per_row, 1), 0) // (per_row // KVH)
    position = lax.broadcasted_iota(jnp.int32, (per_row, span), 1) + member * span
    slot = lax.broadcasted_iota(jnp.int32, (per_row, slots), 1)
    step = lax.broadcasted_iota(jnp.int32, (per_row, slots), 0) % 2
    lane = lax.broadcasted_iota(jnp.int32, (per_row, HD), 1)
    for r in range(rows):
        query = query_s[r * per_row : (r + 1) * per_row, :].astype(jnp.bfloat16)
        query = jnp.concatenate(
            [jnp.where(kv_of == k, query, jnp.zeros_like(query)) for k in range(KVH)], 1
        )

        def product(keys):
            return (
                lax.dot_general(
                    query, keys, (((1,), (1,)), ((), ())), preferred_element_type=jnp.float32
                )
                * scale
            )

        valid = position < lengths_ref[r]
        scores = jnp.where(valid, product(key_ref[r]), FLOOR)
        fresh = (slot % rows == r) & (slot // rows <= step) & (member == 0)
        fresh_scores = jnp.where(fresh, product(new_keys), FLOOR)
        highest = jnp.maximum(
            jnp.max(scores, 1, keepdims=True), jnp.max(fresh_scores, 1, keepdims=True)
        )
        upper = highest.astype(jnp.bfloat16).astype(jnp.float32)
        lower = (highest - upper).astype(jnp.bfloat16).astype(jnp.float32)
        highest = upper + lower
        weights = jnp.where(valid, jnp.exp(scores - highest), 0.0)
        fresh_weights = jnp.where(fresh, jnp.exp(fresh_scores - highest), 0.0)
        total = jnp.sum(weights, 1, keepdims=True) + jnp.sum(fresh_weights, 1, keepdims=True)
        mixed = jnp.dot(
            weights.astype(jnp.bfloat16), value_ref[r], preferred_element_type=jnp.float32
        ) + jnp.dot(
            fresh_weights.astype(jnp.bfloat16), new_values, preferred_element_type=jnp.float32
        )
        own = jnp.zeros((per_row, HD), jnp.float32)
        for k in range(KVH):
            own = jnp.where(kv_of == k, mixed[:, k * HD : (k + 1) * HD], own)
        total_upper = total.astype(jnp.bfloat16).astype(jnp.float32)
        total_lower = total - total_upper
        part = lane // 16 % 4
        facts = jnp.where(
            part < 2,
            jnp.where(part == 0, upper, lower),
            jnp.where(part == 2, total_upper, total_lower),
        )
        facts = jnp.where(lane < 64, facts, pltpu.roll(facts, per_row - 2, 0))
        for t in range(groups):
            message_s[t, pl.ds(r, 4, stride=rows), :] = own[t * 4 : (t + 1) * 4]
            message_s[t, pl.ds(4 * rows + r, 2, stride=rows), :] = facts[t * 4 : t * 4 + 2]
    message_ref[...] = message_s[...].astype(message_ref.dtype)


def merge_kernel(message_ref, attended_ref):
    message = message_ref[...].astype(jnp.float32)
    half = message.shape[1] * 2 // 3
    facts = message[:, half:]

    def fact(i):
        at = (16 * i, 64 + 16 * i)
        return jnp.concatenate([facts[:, :, lane : lane + 1] for lane in at], 1)

    highest, totals = fact(0) + fact(1), fact(2) + fact(3)
    rescale = jnp.exp(highest - jnp.max(highest, 0, keepdims=True))
    total = jnp.sum(totals * rescale, 0)
    mixture = jnp.sum(message[:, :half] * rescale, 0)
    attended = (mixture / total).astype(attended_ref.dtype)
    attended_ref[...] = jnp.concatenate([attended[: half // 2], attended[half // 2 :]], 1)


def total_kernel(terms_ref, after_ref, output_ref):
    output_ref[...] = jnp.sum(terms_ref[...].astype(jnp.float32), 0).astype(output_ref.dtype)


def exchange(blocks, axis):
    return lax.all_to_all(blocks, axis, split_axis=0, concat_axis=0, tiled=True)


def on_device(hidden, norm_gain, qkv_bias, key_cache, value_cache, lengths, fresh_qkv, fresh_out):
    groups = lax.axis_size("tensor")
    replicas = lax.axis_size("dp")
    step_count, row_count, feature_width = hidden.shape
    slots = step_count * row_count
    share = feature_width // replicas
    query_width = QH * HD // groups
    kv_width = KVH * HD // groups
    own_heads = QH // groups
    score_scale = 1.0 / math.sqrt(HD)

    vmem = pl.BlockSpec(memory_space=pltpu.VMEM)
    smem = pl.BlockSpec(memory_space=pltpu.SMEM)
    anywhere = pl.BlockSpec(memory_space=pl.ANY)
    across = [(i, i ^ 4) for i in range(replicas)]
    ahead = [(i, (i & 4) | ((i + 1) & 3)) for i in range(replicas)]
    behind = [(i, (i & 4) | ((i + 3) & 3)) for i in range(replicas)]
    beyond = [(i, (i & 4) | ((i + 2) & 3)) for i in range(replicas)]

    def send(value, pairs):
        return lax.ppermute(value, "dp", pairs)

    group_width = query_width + 2 * kv_width
    own_states, other_states = pl.pallas_call(
        norm_kernel,
        out_shape=(jax.ShapeDtypeStruct((replicas // 2, slots, share), jnp.bfloat16),) * 2,
        compiler_params=pltpu.CompilerParams(vmem_limit_bytes=6 << 20),
        name="norm",
    )(hidden, norm_gain)
    cross_states = send(other_states, across)
    packed = pl.pallas_call(
        lambda *refs: pack_kernel(groups, *refs),
        out_shape=jax.ShapeDtypeStruct((groups, fresh_qkv.shape[0] * 9 // 4, query_width), fresh_qkv.dtype),
        in_specs=[anywhere] + [vmem] * 2,
        compiler_params=pltpu.CompilerParams(vmem_limit_bytes=6 << 20),
        name="pack",
    )(own_states, fresh_qkv, fresh_out)
    packed, cross_states = hold(packed, cross_states)
    packed = exchange(packed, "tensor")

    low_states, far_states, high_states = (
        send(jnp.stack([own_states[k], cross_states[k]]), pairs)
        for k, pairs in ((1, ahead), (2, beyond), (3, behind))
    )
    terms, own_out = pl.pallas_call(
        terms_kernel,
        out_shape=(
            jax.ShapeDtypeStruct((replicas, slots, group_width), jnp.bfloat16),
            jax.ShapeDtypeStruct((share, query_width), packed.dtype),
        ),
        compiler_params=pltpu.CompilerParams(vmem_limit_bytes=8 << 20),
        name="terms",
    )(own_states, cross_states, low_states, high_states, far_states, packed)
    terms = exchange(terms, "dp")
    out_across = send(own_out, across)
    out_low, out_high = send(own_out, ahead), send(own_out, behind)
    own_qkv = pl.pallas_call(
        turn_kernel,
        out_shape=jax.ShapeDtypeStruct((group_width, share), packed.dtype),
        compiler_params=pltpu.CompilerParams(vmem_limit_bytes=4 << 20),
        name="turn",
    )(packed)
    moved = (out_across,)
    projected, out_across = pl.pallas_call(
        lambda terms_ref, bias_ref, *refs: sum_kernel(groups, terms_ref, bias_ref, refs[1]),
        out_shape=(
            jax.ShapeDtypeStruct((groups, slots, group_width), jnp.bfloat16),
            *(jax.ShapeDtypeStruct(v.shape, v.dtype) for v in moved),
        ),
        in_specs=[vmem] * 2 + [anywhere],
        out_specs=(vmem,) + (anywhere,),
        input_output_aliases={2: 1},
        compiler_params=pltpu.CompilerParams(vmem_limit_bytes=3 << 20),
        name="sum",
    )(terms, qkv_bias.reshape(1, group_width), *moved)
    gathered = exchange(projected, "tensor")

    out_cross_low, out_cross_high = send(out_across, ahead), send(out_across, behind)
    qkv_low, qkv_high = send(own_qkv, ahead), send(own_qkv, behind)
    qkv_across = send(own_qkv, across)

    out_shape, qkv_shape = (feature_width, query_width), (group_width, feature_width)

    half_width = HD // 2
    inverse = THETA ** (-jnp.arange(half_width, dtype=jnp.float32) * 2.0 / HD)
    position = (lengths[None, :] + jnp.arange(step_count, dtype=jnp.int32)[:, None]).astype(
        jnp.float32
    )
    angles = position.reshape(slots, 1) * inverse
    cosine, sine = jnp.cos(angles), jnp.sin(angles)
    cosine = jnp.concatenate([cosine, cosine], 1)
    sine = jnp.concatenate([-sine, sine], 1)

    grouped_out = place(
        None, [own_out, out_across], [(0, 0), (1, 0)], 0, out_shape
    )
    grouped_out = place(
        grouped_out, [out_low, out_high], [(0, -1), (0, 1)], 0, out_shape
    )

    message = pl.pallas_call(
        lambda *refs: attend_kernel(score_scale, *refs),
        out_shape=jax.ShapeDtypeStruct((groups, 3 * slots, HD), jnp.bfloat16),
        in_specs=[smem] + [vmem] * 5,
        scratch_shapes=[
            pltpu.VMEM((slots * QH, HD), jnp.float32),
            pltpu.VMEM((groups, 3 * slots, HD), jnp.float32),
        ],
        compiler_params=pltpu.CompilerParams(vmem_limit_bytes=14 << 20),
        name="attend",
    )(lengths, cosine, sine, gathered, key_cache, value_cache)
    message, out_cross_low, out_cross_high, qkv_low, qkv_high, qkv_across, grouped_out = hold(
        message, out_cross_low, out_cross_high, qkv_low, qkv_high, qkv_across, grouped_out
    )
    message = exchange(message, "tensor")
    out_far, out_cross_far = send(out_low, ahead), send(out_cross_high, behind)
    qkv_cross_high = send(qkv_high, across)
    grouped_out = place(
        grouped_out,
        [out_cross_low, out_cross_high],
        [(1, -1), (1, 1)],
        0,
        out_shape,
    )
    grouped_qkv = place(
        None, [own_qkv, qkv_across], [(0, 0), (1, 0)], 1, qkv_shape
    )
    attended = pl.pallas_call(
        merge_kernel,
        out_shape=jax.ShapeDtypeStruct((slots, own_heads * HD), jnp.bfloat16),
        compiler_params=pltpu.CompilerParams(vmem_limit_bytes=3 << 20),
        name="merge",
    )(message)
    grouped_out = place(
        grouped_out,
        [out_far, out_cross_far],
        [(0, 2), (1, 2)],
        0,
        out_shape,
    )
    qkv_far, qkv_cross_far = send(qkv_low, ahead), send(qkv_cross_high, behind)
    qkv_cross_low = send(qkv_low, across)
    grouped_qkv = place(
        grouped_qkv,
        [qkv_low, qkv_high, qkv_cross_high],
        [(0, -1), (0, 1), (1, 1)],
        1,
        qkv_shape,
    )
    grouped_qkv = place(
        grouped_qkv,
        [qkv_far, qkv_cross_low, qkv_cross_far],
        [(0, 2), (1, -1), (1, 2)],
        1,
        qkv_shape,
    )

    term_sums = jnp.dot(attended, grouped_out.T, preferred_element_type=jnp.float32)
    term_sums = term_sums.astype(jnp.bfloat16).reshape(slots, groups, -1).transpose(1, 0, 2)
    term_sums = exchange(term_sums, "tensor")
    attn_output = pl.pallas_call(
        total_kernel,
        out_shape=jax.ShapeDtypeStruct((slots, feature_width // groups), jnp.bfloat16),
        in_specs=[vmem, anywhere],
        compiler_params=pltpu.CompilerParams(vmem_limit_bytes=56 << 20),
        name="total",
    )(term_sums, grouped_qkv)
    attn_output = attn_output.reshape(step_count, row_count, -1)
    return (attn_output, grouped_qkv.T, grouped_out)


def solution(mesh):
    return jax.shard_map(
        on_device,
        mesh=mesh,
        in_specs=(
            P(None, "dp", None),
            P(),
            P("tensor"),
            P("dp", "tensor", None),
            P("dp", "tensor", None),
            P("dp"),
            P(("dp", "tensor"), None),
            P(("dp", "tensor"), None),
        ),
        out_specs=(P(None, "dp", "tensor"), P(None, "tensor"), P(None, "tensor")),
        check_vma=False,
    )
```

```python
import math

import jax
import jax.numpy as jnp
from jax import lax
from jax.experimental import pallas as pl
from jax.experimental.pallas import tpu as pltpu
from jax.sharding import PartitionSpec as P

HD = 128
QH = 32
KVH = 4
THETA = 1000000.0
EPS = 1e-06
FLOOR = -1e30


def pack_kernel(groups, after_ref, qkv_ref, out_ref, packed_ref):
    query_width = QH * HD // groups
    kv_width = KVH * HD // groups
    rows = qkv_ref.shape[0]
    quarter = rows // 4
    for g in range(groups):
        keys_at = QH * HD + g * kv_width
        values_at = QH * HD + KVH * HD + g * kv_width
        at = slice(g * query_width, (g + 1) * query_width)
        packed_ref[g, :rows, :] = qkv_ref[:, at]
        packed_ref[g, rows : 2 * rows, :] = out_ref[:, at]
        pair = jnp.concatenate(
            [
                qkv_ref[:, keys_at : keys_at + kv_width],
                qkv_ref[:, values_at : values_at + kv_width],
            ],
            1,
        )
        packed_ref[g, 2 * rows :, :] = jnp.concatenate(
            [pair[i * quarter : (i + 1) * quarter] for i in range(4)], 1
        )


def unpacked(packed_ref):
    groups, rows, query_width = packed_ref.shape
    rows = rows * 4 // 9
    pair_width = query_width // 4
    queries = jnp.concatenate([packed_ref[t, :rows, :] for t in range(groups)], 0)
    pairs = jnp.concatenate(
        [
            packed_ref[t, 2 * rows :, i * pair_width : (i + 1) * pair_width]
            for t in range(groups)
            for i in range(4)
        ],
        0,
    )
    return queries, pairs


def norm_kernel(states_ref, gain_ref, own_ref, send_ref):
    states = jnp.concatenate([states_ref[0], states_ref[1]], 0).astype(jnp.float32)
    normed = (
        states
        * lax.rsqrt(jnp.mean(states * states, -1, keepdims=True) + EPS)
        * gain_ref[...].reshape(1, -1).astype(jnp.float32)
    ).astype(jnp.bfloat16)
    replica = lax.axis_index("dp")
    column, y_at = replica // 4, replica % 4
    count, _, share = own_ref.shape
    for y in range(count):
        first = normed[:, y * share : (y + 1) * share]
        second = normed[:, (count + y) * share : (count + y + 1) * share]
        slot = (y - y_at) & 3
        own_ref[slot] = jnp.where(column == 0, first, second)
        send_ref[slot] = jnp.where(column == 0, second, first)


def terms_kernel(own, got, low, high, far, packed_ref, terms_ref, out_ref):
    states = jnp.concatenate(
        [own[0], got[0], low[0], low[1], high[0], high[1], far[0], far[1]], 0
    )
    terms = jnp.concatenate(
        [
            jnp.dot(states, weights, preferred_element_type=jnp.float32)
            for weights in unpacked(packed_ref)
        ],
        1,
    ).astype(terms_ref.dtype)
    slots = own.shape[1]
    replica = lax.axis_index("dp")
    order = [(c, y) for y in (0, -1, 1, 2) for c in (0, 1)]
    for i, (c, y) in enumerate(order):
        source = ((replica // 4) ^ c) * 4 + ((replica + y) & 3)
        terms_ref[source] = terms[i * slots : (i + 1) * slots]
    groups, rows, _ = packed_ref.shape
    rows = rows * 4 // 9
    for t in range(groups):
        out_ref[t * rows : (t + 1) * rows] = packed_ref[t, rows : 2 * rows, :]


def hold_kernel(*refs):
    pass


def hold(*values):
    anywhere = pl.BlockSpec(memory_space=pl.ANY)
    return pl.pallas_call(
        hold_kernel,
        out_shape=tuple(jax.ShapeDtypeStruct(v.shape, v.dtype) for v in values),
        in_specs=[anywhere] * len(values),
        out_specs=(anywhere,) * len(values),
        input_output_aliases={i: i for i in range(len(values))},
        compiler_params=pltpu.CompilerParams(vmem_limit_bytes=1 << 20),
        name="hold",
    )(*values)


def sum_kernel(groups, terms_ref, bias_ref, projected_ref):
    total = jnp.sum(terms_ref[...].astype(jnp.float32), 0) + bias_ref[...].astype(jnp.float32)
    total = total.astype(projected_ref.dtype)
    for g in range(groups):
        projected_ref[g] = total


def turn_kernel(packed_ref, turned_ref):
    queries, pairs = unpacked(packed_ref)
    width = queries.shape[1]
    turned_ref[:width] = queries.T
    turned_ref[width:] = pairs.T


def place_kernel(axis, where, mark, *refs):
    parts = refs[: len(where)]
    replica = lax.axis_index("dp")
    whole_ref, sems = refs[-2:]
    if mark:
        whole_ref, mark_ref, sems = refs[-3:]
        mark_ref[...] = jnp.zeros_like(mark_ref)
    copies = []
    for i, (part, (c, y)) in enumerate(zip(parts, where)):
        size = part.shape[axis]
        source = ((replica // 4) ^ c) * 4 + ((replica + y) & 3)
        at = pl.ds(pl.multiple_of(source * size, size), size)
        target = whole_ref.at[at, :] if axis == 0 else whole_ref.at[:, at]
        copies.append(pltpu.make_async_copy(part, target, sems.at[i]))
    for copy in copies:
        copy.start()
    for copy in copies:
        copy.wait()


def place(whole, parts, where, axis, shape, mark=False):
    count = len(parts)
    continued = whole is not None
    whole_shape = jax.ShapeDtypeStruct(shape, parts[0].dtype)
    vmem = pl.BlockSpec(memory_space=pltpu.VMEM)
    anywhere = pl.BlockSpec(memory_space=pl.ANY)
    return pl.pallas_call(
        lambda *refs: place_kernel(axis, where, mark, *refs),
        out_shape=(whole_shape, jax.ShapeDtypeStruct((8, 128), jnp.float32))
        if mark
        else whole_shape,
        in_specs=[vmem] * count + ([anywhere] if continued else []),
        out_specs=(anywhere, vmem) if mark else anywhere,
        scratch_shapes=[pltpu.SemaphoreType.DMA((count,))],
        input_output_aliases={count: 0} if continued else {},
        compiler_params=pltpu.CompilerParams(vmem_limit_bytes=4 << 20),
        name="place",
    )(*parts, *((whole,) if continued else ()))


def attend_kernel(scale, lengths_ref, cosine_ref, sine_ref, new_ref, key_ref, value_ref, message_ref, query_s, message_s):
    groups, slots, _ = new_ref.shape
    rows, span, _ = key_ref.shape
    per_row = query_s.shape[0] // rows
    cosine, sine = cosine_ref[...], sine_ref[...]

    def turned(values):
        values = values.astype(jnp.float32)
        return values * cosine + pltpu.roll(values, HD // 2, 1) * sine

    for t in range(groups):
        for j in range(2):
            query = turned(new_ref[t, :, j * HD : (j + 1) * HD])
            for s in range(2):
                query_s[pl.ds(t * 4 + j * 2 + s, rows, stride=per_row), :] = query[
                    s * rows : (s + 1) * rows
                ]
    start, width = 2 * HD, KVH * HD // groups
    new_keys = jnp.concatenate([new_ref[t, :, start : start + width] for t in range(groups)], 1)
    new_keys = jnp.concatenate(
        [turned(new_keys[:, k * HD : (k + 1) * HD]) for k in range(KVH)], 1
    ).astype(jnp.bfloat16)
    new_values = jnp.concatenate(
        [new_ref[t, :, start + width : start + 2 * width] for t in range(groups)], 1
    )

    member = lax.axis_index("tensor")
    kv_of = lax.broadcasted_iota(jnp.int32, (per_row, 1), 0) // (per_row // KVH)
    position = lax.broadcasted_iota(jnp.int32, (per_row, span), 1) + member * span
    slot = lax.broadcasted_iota(jnp.int32, (per_row, slots), 1)
    step = lax.broadcasted_iota(jnp.int32, (per_row, slots), 0) % 2
    lane = lax.broadcasted_iota(jnp.int32, (per_row, HD), 1)
    for r in range(rows):
        query = query_s[r * per_row : (r + 1) * per_row, :].astype(jnp.bfloat16)
        query = jnp.concatenate(
            [jnp.where(kv_of == k, query, jnp.zeros_like(query)) for k in range(KVH)], 1
        )

        def product(keys):
            return (
                lax.dot_general(
                    query, keys, (((1,), (1,)), ((), ())), preferred_element_type=jnp.float32
                )
                * scale
            )

        valid = position < lengths_ref[r]
        scores = jnp.where(valid, product(key_ref[r]), FLOOR)
        fresh = (slot % rows == r) & (slot // rows <= step) & (member == 0)
        fresh_scores = jnp.where(fresh, product(new_keys), FLOOR)
        highest = jnp.maximum(
            jnp.max(scores, 1, keepdims=True), jnp.max(fresh_scores, 1, keepdims=True)
        )
        upper = highest.astype(jnp.bfloat16).astype(jnp.float32)
        lower = (highest - upper).astype(jnp.bfloat16).astype(jnp.float32)
        highest = upper + lower
        weights = jnp.where(valid, jnp.exp(scores - highest), 0.0)
        fresh_weights = jnp.where(fresh, jnp.exp(fresh_scores - highest), 0.0)
        total = jnp.sum(weights, 1, keepdims=True) + jnp.sum(fresh_weights, 1, keepdims=True)
        mixed = jnp.dot(
            weights.astype(jnp.bfloat16), value_ref[r], preferred_element_type=jnp.float32
        ) + jnp.dot(
            fresh_weights.astype(jnp.bfloat16), new_values, preferred_element_type=jnp.float32
        )
        own = jnp.zeros((per_row, HD), jnp.float32)
        for k in range(KVH):
            own = jnp.where(kv_of == k, mixed[:, k * HD : (k + 1) * HD], own)
        total_upper = total.astype(jnp.bfloat16).astype(jnp.float32)
        total_lower = total - total_upper
        part = lane // 16 % 4
        facts = jnp.where(
            part < 2,
            jnp.where(part == 0, upper, lower),
            jnp.where(part == 2, total_upper, total_lower),
        )
        facts = jnp.where(lane < 64, facts, pltpu.roll(facts, per_row - 2, 0))
        for t in range(groups):
            message_s[t, pl.ds(r, 4, stride=rows), :] = own[t * 4 : (t + 1) * 4]
            message_s[t, pl.ds(4 * rows + r, 2, stride=rows), :] = facts[t * 4 : t * 4 + 2]
    message_ref[...] = message_s[...].astype(message_ref.dtype)


def merge_kernel(message_ref, attended_ref):
    message = message_ref[...].astype(jnp.float32)
    half = message.shape[1] * 2 // 3
    facts = message[:, half:]

    def fact(i):
        at = (16 * i, 64 + 16 * i)
        return jnp.concatenate([facts[:, :, lane : lane + 1] for lane in at], 1)

    highest, totals = fact(0) + fact(1), fact(2) + fact(3)
    rescale = jnp.exp(highest - jnp.max(highest, 0, keepdims=True))
    total = jnp.sum(totals * rescale, 0)
    mixture = jnp.sum(message[:, :half] * rescale, 0)
    attended = (mixture / total).astype(attended_ref.dtype)
    attended_ref[...] = jnp.concatenate([attended[: half // 2], attended[half // 2 :]], 1)


def total_kernel(terms_ref, after_ref, output_ref):
    output_ref[...] = jnp.sum(terms_ref[...].astype(jnp.float32), 0).astype(output_ref.dtype)


def exchange(blocks, axis):
    return lax.all_to_all(blocks, axis, split_axis=0, concat_axis=0, tiled=True)


def on_device(hidden, norm_gain, qkv_bias, key_cache, value_cache, lengths, fresh_qkv, fresh_out):
    groups = lax.axis_size("tensor")
    replicas = lax.axis_size("dp")
    step_count, row_count, feature_width = hidden.shape
    slots = step_count * row_count
    share = feature_width // replicas
    query_width = QH * HD // groups
    kv_width = KVH * HD // groups
    own_heads = QH // groups
    score_scale = 1.0 / math.sqrt(HD)

    vmem = pl.BlockSpec(memory_space=pltpu.VMEM)
    smem = pl.BlockSpec(memory_space=pltpu.SMEM)
    anywhere = pl.BlockSpec(memory_space=pl.ANY)
    across = [(i, i ^ 4) for i in range(replicas)]
    ahead = [(i, (i & 4) | ((i + 1) & 3)) for i in range(replicas)]
    behind = [(i, (i & 4) | ((i + 3) & 3)) for i in range(replicas)]
    beyond = [(i, (i & 4) | ((i + 2) & 3)) for i in range(replicas)]

    def send(value, pairs):
        return lax.ppermute(value, "dp", pairs)

    group_width = query_width + 2 * kv_width
    own_states, other_states = pl.pallas_call(
        norm_kernel,
        out_shape=(jax.ShapeDtypeStruct((replicas // 2, slots, share), jnp.bfloat16),) * 2,
        compiler_params=pltpu.CompilerParams(vmem_limit_bytes=6 << 20),
        name="norm",
    )(hidden, norm_gain)
    cross_states = send(other_states, across)
    packed = pl.pallas_call(
        lambda *refs: pack_kernel(groups, *refs),
        out_shape=jax.ShapeDtypeStruct((groups, fresh_qkv.shape[0] * 9 // 4, query_width), fresh_qkv.dtype),
        in_specs=[anywhere] + [vmem] * 2,
        compiler_params=pltpu.CompilerParams(vmem_limit_bytes=6 << 20),
        name="pack",
    )(own_states, fresh_qkv, fresh_out)
    packed, cross_states = hold(packed, cross_states)
    packed = exchange(packed, "tensor")

    low_states, far_states, high_states = (
        send(jnp.stack([own_states[k], cross_states[k]]), pairs)
        for k, pairs in ((1, ahead), (2, beyond), (3, behind))
    )
    terms, own_out = pl.pallas_call(
        terms_kernel,
        out_shape=(
            jax.ShapeDtypeStruct((replicas, slots, group_width), jnp.bfloat16),
            jax.ShapeDtypeStruct((share, query_width), packed.dtype),
        ),
        compiler_params=pltpu.CompilerParams(vmem_limit_bytes=8 << 20),
        name="terms",
    )(own_states, cross_states, low_states, high_states, far_states, packed)
    terms = exchange(terms, "dp")
    out_across = send(own_out, across)
    out_low, out_high = send(own_out, ahead), send(own_out, behind)
    own_qkv = pl.pallas_call(
        turn_kernel,
        out_shape=jax.ShapeDtypeStruct((group_width, share), packed.dtype),
        compiler_params=pltpu.CompilerParams(vmem_limit_bytes=4 << 20),
        name="turn",
    )(packed)
    moved = (out_across,)
    projected, out_across = pl.pallas_call(
        lambda terms_ref, bias_ref, *refs: sum_kernel(groups, terms_ref, bias_ref, refs[1]),
        out_shape=(
            jax.ShapeDtypeStruct((groups, slots, group_width), jnp.bfloat16),
            *(jax.ShapeDtypeStruct(v.shape, v.dtype) for v in moved),
        ),
        in_specs=[vmem] * 2 + [anywhere],
        out_specs=(vmem,) + (anywhere,),
        input_output_aliases={2: 1},
        compiler_params=pltpu.CompilerParams(vmem_limit_bytes=3 << 20),
        name="sum",
    )(terms, qkv_bias.reshape(1, group_width), *moved)
    gathered = exchange(projected, "tensor")

    out_cross_low, out_cross_high = send(out_across, ahead), send(out_across, behind)
    qkv_low, qkv_high = send(own_qkv, ahead), send(own_qkv, behind)
    qkv_across = send(own_qkv, across)

    out_shape, qkv_shape = (feature_width, query_width), (group_width, feature_width)

    half_width = HD // 2
    inverse = THETA ** (-jnp.arange(half_width, dtype=jnp.float32) * 2.0 / HD)
    position = (lengths[None, :] + jnp.arange(step_count, dtype=jnp.int32)[:, None]).astype(
        jnp.float32
    )
    angles = position.reshape(slots, 1) * inverse
    cosine, sine = jnp.cos(angles), jnp.sin(angles)
    cosine = jnp.concatenate([cosine, cosine], 1)
    sine = jnp.concatenate([-sine, sine], 1)

    grouped_out = place(
        None, [own_out, out_across], [(0, 0), (1, 0)], 0, out_shape
    )
    grouped_out = place(
        grouped_out, [out_low, out_high], [(0, -1), (0, 1)], 0, out_shape
    )

    message = pl.pallas_call(
        lambda *refs: attend_kernel(score_scale, *refs),
        out_shape=jax.ShapeDtypeStruct((groups, 3 * slots, HD), jnp.bfloat16),
        in_specs=[smem] + [vmem] * 5,
        scratch_shapes=[
            pltpu.VMEM((slots * QH, HD), jnp.float32),
            pltpu.VMEM((groups, 3 * slots, HD), jnp.float32),
        ],
        compiler_params=pltpu.CompilerParams(vmem_limit_bytes=14 << 20),
        name="attend",
    )(lengths, cosine, sine, gathered, key_cache, value_cache)
    message, out_cross_low, out_cross_high, qkv_low, qkv_high, qkv_across, grouped_out = hold(
        message, out_cross_low, out_cross_high, qkv_low, qkv_high, qkv_across, grouped_out
    )
    message = exchange(message, "tensor")
    out_far, out_cross_far = send(out_low, ahead), send(out_cross_high, behind)
    qkv_cross_high = send(qkv_high, across)
    grouped_out = place(
        grouped_out,
        [out_cross_low, out_cross_high],
        [(1, -1), (1, 1)],
        0,
        out_shape,
    )
    grouped_qkv = place(
        None, [own_qkv, qkv_across], [(0, 0), (1, 0)], 1, qkv_shape
    )
    attended = pl.pallas_call(
        merge_kernel,
        out_shape=jax.ShapeDtypeStruct((slots, own_heads * HD), jnp.bfloat16),
        compiler_params=pltpu.CompilerParams(vmem_limit_bytes=3 << 20),
        name="merge",
    )(message)
    grouped_out = place(
        grouped_out,
        [out_far, out_cross_far],
        [(0, 2), (1, 2)],
        0,
        out_shape,
    )
    qkv_far, qkv_cross_far = send(qkv_low, ahead), send(qkv_cross_high, behind)
    qkv_cross_low = send(qkv_low, across)
    grouped_qkv = place(
        grouped_qkv,
        [qkv_low, qkv_high, qkv_cross_high],
        [(0, -1), (0, 1), (1, 1)],
        1,
        qkv_shape,
    )
    grouped_qkv, placed = place(
        grouped_qkv,
        [qkv_far, qkv_cross_low, qkv_cross_far],
        [(0, 2), (1, -1), (1, 2)],
        1,
        qkv_shape,
        mark=True,
    )

    term_sums = jnp.dot(attended, grouped_out.T, preferred_element_type=jnp.float32)
    term_sums = term_sums.astype(jnp.bfloat16).reshape(slots, groups, -1).transpose(1, 0, 2)
    term_sums = exchange(term_sums, "tensor")
    attn_output = pl.pallas_call(
        total_kernel,
        out_shape=jax.ShapeDtypeStruct((slots, feature_width // groups), jnp.bfloat16),
        in_specs=[vmem, anywhere],
        compiler_params=pltpu.CompilerParams(vmem_limit_bytes=2 << 20),
        name="total",
    )(term_sums, placed)
    attn_output = attn_output.reshape(step_count, row_count, -1)
    return (attn_output, grouped_qkv.T, grouped_out)


def solution(mesh):
    return jax.shard_map(
        on_device,
        mesh=mesh,
        in_specs=(
            P(None, "dp", None),
            P(),
            P("tensor"),
            P("dp", "tensor", None),
            P("dp", "tensor", None),
            P("dp"),
            P(("dp", "tensor"), None),
            P(("dp", "tensor"), None),
        ),
        out_specs=(P(None, "dp", "tensor"), P(None, "tensor"), P(None, "tensor")),
        check_vma=False,
    )
```

```python
import math

import jax
import jax.numpy as jnp
from jax import lax
from jax.experimental import pallas as pl
from jax.experimental.pallas import tpu as pltpu
from jax.sharding import PartitionSpec as P

HD = 128
QH = 32
KVH = 4
THETA = 1000000.0
EPS = 1e-06
FLOOR = -1e30


def pack_kernel(groups, after_ref, qkv_in, out_in, packed_ref, qkv_ref, out_ref, sems):
    query_width = QH * HD // groups
    kv_width = KVH * HD // groups
    rows = qkv_ref.shape[0]
    quarter = rows // 4
    copies = []
    for i, (source, target) in enumerate(((qkv_in, qkv_ref), (out_in, out_ref))):
        copies.append(pltpu.make_async_copy(source, target, sems.at[i]))
    for copy in copies:
        copy.start()
    for copy in copies:
        copy.wait()
    for g in range(groups):
        keys_at = QH * HD + g * kv_width
        values_at = QH * HD + KVH * HD + g * kv_width
        at = slice(g * query_width, (g + 1) * query_width)
        packed_ref[g, :rows, :] = qkv_ref[:, at]
        packed_ref[g, rows : 2 * rows, :] = out_ref[:, at]
        pair = jnp.concatenate(
            [
                qkv_ref[:, keys_at : keys_at + kv_width],
                qkv_ref[:, values_at : values_at + kv_width],
            ],
            1,
        )
        packed_ref[g, 2 * rows :, :] = jnp.concatenate(
            [pair[i * quarter : (i + 1) * quarter] for i in range(4)], 1
        )


def unpacked(packed_ref):
    groups, rows, query_width = packed_ref.shape
    rows = rows * 4 // 9
    pair_width = query_width // 4
    queries = jnp.concatenate([packed_ref[t, :rows, :] for t in range(groups)], 0)
    pairs = jnp.concatenate(
        [
            packed_ref[t, 2 * rows :, i * pair_width : (i + 1) * pair_width]
            for t in range(groups)
            for i in range(4)
        ],
        0,
    )
    return queries, pairs


def norm_kernel(states_in, gain_in, own_ref, send_ref, states_ref, gain_ref, sems):
    copies = [
        pltpu.make_async_copy(states_in, states_ref, sems.at[0]),
        pltpu.make_async_copy(gain_in, gain_ref, sems.at[1]),
    ]
    for copy in copies:
        copy.start()
    for copy in copies:
        copy.wait()
    states = jnp.concatenate([states_ref[0], states_ref[1]], 0).astype(jnp.float32)
    normed = (
        states
        * lax.rsqrt(jnp.mean(states * states, -1, keepdims=True) + EPS)
        * gain_ref[...].reshape(1, -1).astype(jnp.float32)
    ).astype(jnp.bfloat16)
    replica = lax.axis_index("dp")
    column, y_at = replica // 4, replica % 4
    count, _, share = own_ref.shape
    for y in range(count):
        first = normed[:, y * share : (y + 1) * share]
        second = normed[:, (count + y) * share : (count + y + 1) * share]
        slot = (y - y_at) & 3
        own_ref[slot] = jnp.where(column == 0, first, second)
        send_ref[slot] = jnp.where(column == 0, second, first)


def terms_kernel(own, got, low, high, far, packed_ref, terms_ref, out_ref):
    states = jnp.concatenate(
        [own[0], got[0], low[0], low[1], high[0], high[1], far[0], far[1]], 0
    )
    terms = jnp.concatenate(
        [
            jnp.dot(states, weights, preferred_element_type=jnp.float32)
            for weights in unpacked(packed_ref)
        ],
        1,
    ).astype(terms_ref.dtype)
    slots = own.shape[1]
    replica = lax.axis_index("dp")
    order = [(c, y) for y in (0, -1, 1, 2) for c in (0, 1)]
    for i, (c, y) in enumerate(order):
        source = ((replica // 4) ^ c) * 4 + ((replica + y) & 3)
        terms_ref[source] = terms[i * slots : (i + 1) * slots]
    groups, rows, _ = packed_ref.shape
    rows = rows * 4 // 9
    for t in range(groups):
        out_ref[t * rows : (t + 1) * rows] = packed_ref[t, rows : 2 * rows, :]


def hold_kernel(*refs):
    pass


def hold(*values):
    anywhere = pl.BlockSpec(memory_space=pl.ANY)
    return pl.pallas_call(
        hold_kernel,
        out_shape=tuple(jax.ShapeDtypeStruct(v.shape, v.dtype) for v in values),
        in_specs=[anywhere] * len(values),
        out_specs=(anywhere,) * len(values),
        input_output_aliases={i: i for i in range(len(values))},
        compiler_params=pltpu.CompilerParams(vmem_limit_bytes=1 << 20),
        name="hold",
    )(*values)


def sum_kernel(groups, terms_ref, bias_ref, projected_ref):
    total = jnp.sum(terms_ref[...].astype(jnp.float32), 0) + bias_ref[...].astype(jnp.float32)
    total = total.astype(projected_ref.dtype)
    for g in range(groups):
        projected_ref[g] = total


def turn_kernel(packed_ref, turned_ref):
    queries, pairs = unpacked(packed_ref)
    width = queries.shape[1]
    turned_ref[:width] = queries.T
    turned_ref[width:] = pairs.T


def place_kernel(axis, where, mark, *refs):
    parts = refs[: len(where)]
    replica = lax.axis_index("dp")
    whole_ref, sems = refs[-2:]
    if mark:
        whole_ref, mark_ref, sems = refs[-3:]
        mark_ref[...] = jnp.zeros_like(mark_ref)
    copies = []
    for i, (part, (c, y)) in enumerate(zip(parts, where)):
        size = part.shape[axis]
        source = ((replica // 4) ^ c) * 4 + ((replica + y) & 3)
        at = pl.ds(pl.multiple_of(source * size, size), size)
        target = whole_ref.at[at, :] if axis == 0 else whole_ref.at[:, at]
        copies.append(pltpu.make_async_copy(part, target, sems.at[i]))
    for copy in copies:
        copy.start()
    for copy in copies:
        copy.wait()


def place(whole, parts, where, axis, shape, mark=False):
    count = len(parts)
    continued = whole is not None
    whole_shape = jax.ShapeDtypeStruct(shape, parts[0].dtype)
    vmem = pl.BlockSpec(memory_space=pltpu.VMEM)
    anywhere = pl.BlockSpec(memory_space=pl.ANY)
    return pl.pallas_call(
        lambda *refs: place_kernel(axis, where, mark, *refs),
        out_shape=(whole_shape, jax.ShapeDtypeStruct((8, 128), jnp.float32))
        if mark
        else whole_shape,
        in_specs=[vmem] * count + ([anywhere] if continued else []),
        out_specs=(anywhere, vmem) if mark else anywhere,
        scratch_shapes=[pltpu.SemaphoreType.DMA((count,))],
        input_output_aliases={count: 0} if continued else {},
        compiler_params=pltpu.CompilerParams(vmem_limit_bytes=4 << 20),
        name="place",
    )(*parts, *((whole,) if continued else ()))


def attend_kernel(scale, lengths_ref, cosine_ref, sine_ref, new_ref, key_ref, value_ref, message_ref, query_s, message_s, key_s, value_s, sems):
    groups, slots, _ = new_ref.shape
    rows, span, _ = key_ref.shape
    per_row = query_s.shape[0] // rows
    key_copies, value_copies = (
        [
            pltpu.make_async_copy(
                ref.at[pl.ds(r, 4)], scratch.at[pl.ds(r, 4)], sems.at[i, r]
            )
            for r in range(0, rows, 4)
        ]
        for i, (ref, scratch) in enumerate(((key_ref, key_s), (value_ref, value_s)))
    )
    for key_copy, value_copy in zip(key_copies, value_copies):
        key_copy.start()
        value_copy.start()
    cosine, sine = cosine_ref[...], sine_ref[...]

    def turned(values):
        values = values.astype(jnp.float32)
        return values * cosine + pltpu.roll(values, HD // 2, 1) * sine

    for t in range(groups):
        for j in range(2):
            query = turned(new_ref[t, :, j * HD : (j + 1) * HD])
            for s in range(2):
                query_s[pl.ds(t * 4 + j * 2 + s, rows, stride=per_row), :] = query[
                    s * rows : (s + 1) * rows
                ]
    start, width = 2 * HD, KVH * HD // groups
    new_keys = jnp.concatenate([new_ref[t, :, start : start + width] for t in range(groups)], 1)
    new_keys = jnp.concatenate(
        [turned(new_keys[:, k * HD : (k + 1) * HD]) for k in range(KVH)], 1
    ).astype(jnp.bfloat16)
    new_values = jnp.concatenate(
        [new_ref[t, :, start + width : start + 2 * width] for t in range(groups)], 1
    )

    member = lax.axis_index("tensor")
    kv_of = lax.broadcasted_iota(jnp.int32, (per_row, 1), 0) // (per_row // KVH)
    position = lax.broadcasted_iota(jnp.int32, (per_row, span), 1) + member * span
    slot = lax.broadcasted_iota(jnp.int32, (per_row, slots), 1)
    step = lax.broadcasted_iota(jnp.int32, (per_row, slots), 0) % 2
    lane = lax.broadcasted_iota(jnp.int32, (per_row, HD), 1)
    for r in range(rows):
        query = query_s[r * per_row : (r + 1) * per_row, :].astype(jnp.bfloat16)
        query = jnp.concatenate(
            [jnp.where(kv_of == k, query, jnp.zeros_like(query)) for k in range(KVH)], 1
        )

        def product(keys):
            return (
                lax.dot_general(
                    query, keys, (((1,), (1,)), ((), ())), preferred_element_type=jnp.float32
                )
                * scale
            )

        valid = position < lengths_ref[r]
        if r % 4 == 0:
            key_copies[r // 4].wait()
        scores = jnp.where(valid, product(key_s[r]), FLOOR)
        fresh = (slot % rows == r) & (slot // rows <= step) & (member == 0)
        fresh_scores = jnp.where(fresh, product(new_keys), FLOOR)
        highest = jnp.maximum(
            jnp.max(scores, 1, keepdims=True), jnp.max(fresh_scores, 1, keepdims=True)
        )
        upper = highest.astype(jnp.bfloat16).astype(jnp.float32)
        lower = (highest - upper).astype(jnp.bfloat16).astype(jnp.float32)
        highest = upper + lower
        weights = jnp.where(valid, jnp.exp(scores - highest), 0.0)
        fresh_weights = jnp.where(fresh, jnp.exp(fresh_scores - highest), 0.0)
        total = jnp.sum(weights, 1, keepdims=True) + jnp.sum(fresh_weights, 1, keepdims=True)
        if r % 4 == 0:
            value_copies[r // 4].wait()
        mixed = jnp.dot(
            weights.astype(jnp.bfloat16), value_s[r], preferred_element_type=jnp.float32
        ) + jnp.dot(
            fresh_weights.astype(jnp.bfloat16), new_values, preferred_element_type=jnp.float32
        )
        own = jnp.zeros((per_row, HD), jnp.float32)
        for k in range(KVH):
            own = jnp.where(kv_of == k, mixed[:, k * HD : (k + 1) * HD], own)
        total_upper = total.astype(jnp.bfloat16).astype(jnp.float32)
        total_lower = total - total_upper
        part = lane // 16 % 4
        facts = jnp.where(
            part < 2,
            jnp.where(part == 0, upper, lower),
            jnp.where(part == 2, total_upper, total_lower),
        )
        facts = jnp.where(lane < 64, facts, pltpu.roll(facts, per_row - 2, 0))
        for t in range(groups):
            message_s[t, pl.ds(r, 4, stride=rows), :] = own[t * 4 : (t + 1) * 4]
            message_s[t, pl.ds(4 * rows + r, 2, stride=rows), :] = facts[t * 4 : t * 4 + 2]
    message_ref[...] = message_s[...].astype(message_ref.dtype)


def merge_kernel(message_ref, attended_ref):
    message = message_ref[...].astype(jnp.float32)
    half = message.shape[1] * 2 // 3
    facts = message[:, half:]

    def fact(i):
        at = (16 * i, 64 + 16 * i)
        return jnp.concatenate([facts[:, :, lane : lane + 1] for lane in at], 1)

    highest, totals = fact(0) + fact(1), fact(2) + fact(3)
    rescale = jnp.exp(highest - jnp.max(highest, 0, keepdims=True))
    total = jnp.sum(totals * rescale, 0)
    mixture = jnp.sum(message[:, :half] * rescale, 0)
    attended = (mixture / total).astype(attended_ref.dtype)
    attended_ref[...] = jnp.concatenate([attended[: half // 2], attended[half // 2 :]], 1)


def total_kernel(terms_ref, after_ref, output_ref):
    output_ref[...] = jnp.sum(terms_ref[...].astype(jnp.float32), 0).astype(output_ref.dtype)


def exchange(blocks, axis):
    return lax.all_to_all(blocks, axis, split_axis=0, concat_axis=0, tiled=True)


def on_device(hidden, norm_gain, qkv_bias, key_cache, value_cache, lengths, fresh_qkv, fresh_out):
    groups = lax.axis_size("tensor")
    replicas = lax.axis_size("dp")
    step_count, row_count, feature_width = hidden.shape
    slots = step_count * row_count
    share = feature_width // replicas
    query_width = QH * HD // groups
    kv_width = KVH * HD // groups
    own_heads = QH // groups
    score_scale = 1.0 / math.sqrt(HD)

    vmem = pl.BlockSpec(memory_space=pltpu.VMEM)
    smem = pl.BlockSpec(memory_space=pltpu.SMEM)
    anywhere = pl.BlockSpec(memory_space=pl.ANY)
    in_hbm = pl.BlockSpec(memory_space=pltpu.HBM)

    def stay(value):
        return pltpu.with_memory_space_constraint(value, pltpu.HBM)

    across = [(i, i ^ 4) for i in range(replicas)]
    ahead = [(i, (i & 4) | ((i + 1) & 3)) for i in range(replicas)]
    behind = [(i, (i & 4) | ((i + 3) & 3)) for i in range(replicas)]
    beyond = [(i, (i & 4) | ((i + 2) & 3)) for i in range(replicas)]

    def send(value, pairs):
        return lax.ppermute(value, "dp", pairs)

    group_width = query_width + 2 * kv_width
    own_states, other_states = pl.pallas_call(
        norm_kernel,
        out_shape=(jax.ShapeDtypeStruct((replicas // 2, slots, share), jnp.bfloat16),) * 2,
        in_specs=[in_hbm] * 2,
        scratch_shapes=[
            pltpu.VMEM(hidden.shape, hidden.dtype),
            pltpu.VMEM(norm_gain.shape, norm_gain.dtype),
            pltpu.SemaphoreType.DMA((2,)),
        ],
        compiler_params=pltpu.CompilerParams(vmem_limit_bytes=6 << 20),
        name="norm",
    )(stay(hidden), stay(norm_gain))
    cross_states = send(other_states, across)
    packed = pl.pallas_call(
        lambda *refs: pack_kernel(groups, *refs),
        out_shape=jax.ShapeDtypeStruct((groups, fresh_qkv.shape[0] * 9 // 4, query_width), fresh_qkv.dtype),
        in_specs=[anywhere] + [in_hbm] * 2,
        scratch_shapes=[
            pltpu.VMEM(fresh_qkv.shape, fresh_qkv.dtype),
            pltpu.VMEM(fresh_out.shape, fresh_out.dtype),
            pltpu.SemaphoreType.DMA((2,)),
        ],
        compiler_params=pltpu.CompilerParams(vmem_limit_bytes=6 << 20),
        name="pack",
    )(own_states, stay(fresh_qkv), stay(fresh_out))
    packed, cross_states = hold(packed, cross_states)
    packed = exchange(packed, "tensor")

    low_states, far_states, high_states = (
        send(jnp.stack([own_states[k], cross_states[k]]), pairs)
        for k, pairs in ((1, ahead), (2, beyond), (3, behind))
    )
    terms, own_out = pl.pallas_call(
        terms_kernel,
        out_shape=(
            jax.ShapeDtypeStruct((replicas, slots, group_width), jnp.bfloat16),
            jax.ShapeDtypeStruct((share, query_width), packed.dtype),
        ),
        compiler_params=pltpu.CompilerParams(vmem_limit_bytes=8 << 20),
        name="terms",
    )(own_states, cross_states, low_states, high_states, far_states, packed)
    terms = exchange(terms, "dp")
    out_across = send(own_out, across)
    out_low, out_high = send(own_out, ahead), send(own_out, behind)
    own_qkv = pl.pallas_call(
        turn_kernel,
        out_shape=jax.ShapeDtypeStruct((group_width, share), packed.dtype),
        compiler_params=pltpu.CompilerParams(vmem_limit_bytes=4 << 20),
        name="turn",
    )(packed)
    moved = (out_across,)
    projected, out_across = pl.pallas_call(
        lambda terms_ref, bias_ref, *refs: sum_kernel(groups, terms_ref, bias_ref, refs[1]),
        out_shape=(
            jax.ShapeDtypeStruct((groups, slots, group_width), jnp.bfloat16),
            *(jax.ShapeDtypeStruct(v.shape, v.dtype) for v in moved),
        ),
        in_specs=[vmem] * 2 + [in_hbm],
        out_specs=(vmem, in_hbm),
        input_output_aliases={2: 1},
        compiler_params=pltpu.CompilerParams(vmem_limit_bytes=3 << 20),
        name="sum",
    )(terms, qkv_bias.reshape(1, group_width), stay(out_across))
    gathered = exchange(projected, "tensor")

    out_cross_low, out_cross_high = send(out_across, ahead), send(out_across, behind)
    qkv_low, qkv_high = send(own_qkv, ahead), send(own_qkv, behind)
    qkv_across = send(own_qkv, across)

    out_shape, qkv_shape = (feature_width, query_width), (group_width, feature_width)

    half_width = HD // 2
    inverse = THETA ** (-jnp.arange(half_width, dtype=jnp.float32) * 2.0 / HD)
    position = (lengths[None, :] + jnp.arange(step_count, dtype=jnp.int32)[:, None]).astype(
        jnp.float32
    )
    angles = position.reshape(slots, 1) * inverse
    cosine, sine = jnp.cos(angles), jnp.sin(angles)
    cosine = jnp.concatenate([cosine, cosine], 1)
    sine = jnp.concatenate([-sine, sine], 1)

    grouped_out = place(
        None, [own_out, out_across], [(0, 0), (1, 0)], 0, out_shape
    )
    grouped_out = place(
        grouped_out, [out_low, out_high], [(0, -1), (0, 1)], 0, out_shape
    )

    message = pl.pallas_call(
        lambda *refs: attend_kernel(score_scale, *refs),
        out_shape=jax.ShapeDtypeStruct((groups, 3 * slots, HD), jnp.bfloat16),
        in_specs=[smem] + [vmem] * 3 + [in_hbm] * 2,
        scratch_shapes=[
            pltpu.VMEM((slots * QH, HD), jnp.float32),
            pltpu.VMEM((groups, 3 * slots, HD), jnp.float32),
            pltpu.VMEM(key_cache.shape, key_cache.dtype),
            pltpu.VMEM(value_cache.shape, value_cache.dtype),
            pltpu.SemaphoreType.DMA((2, row_count)),
        ],
        compiler_params=pltpu.CompilerParams(vmem_limit_bytes=14 << 20),
        name="attend",
    )(lengths, cosine, sine, gathered, stay(key_cache), stay(value_cache))
    message, out_cross_low, out_cross_high, qkv_low, qkv_high, qkv_across, grouped_out = hold(
        message, out_cross_low, out_cross_high, qkv_low, qkv_high, qkv_across, grouped_out
    )
    message = exchange(message, "tensor")
    out_far, out_cross_far = send(out_low, ahead), send(out_cross_high, behind)
    qkv_cross_high = send(qkv_high, across)
    grouped_out = place(
        grouped_out,
        [out_cross_low, out_cross_high],
        [(1, -1), (1, 1)],
        0,
        out_shape,
    )
    grouped_qkv = place(
        None, [own_qkv, qkv_across], [(0, 0), (1, 0)], 1, qkv_shape
    )
    attended = pl.pallas_call(
        merge_kernel,
        out_shape=jax.ShapeDtypeStruct((slots, own_heads * HD), jnp.bfloat16),
        compiler_params=pltpu.CompilerParams(vmem_limit_bytes=3 << 20),
        name="merge",
    )(message)
    grouped_out = place(
        grouped_out,
        [out_far, out_cross_far],
        [(0, 2), (1, 2)],
        0,
        out_shape,
    )
    qkv_far, qkv_cross_far = send(qkv_low, ahead), send(qkv_cross_high, behind)
    qkv_cross_low = send(qkv_low, across)
    grouped_qkv = place(
        grouped_qkv,
        [qkv_low, qkv_high, qkv_cross_high],
        [(0, -1), (0, 1), (1, 1)],
        1,
        qkv_shape,
    )
    grouped_qkv, placed = place(
        grouped_qkv,
        [qkv_far, qkv_cross_low, qkv_cross_far],
        [(0, 2), (1, -1), (1, 2)],
        1,
        qkv_shape,
        mark=True,
    )

    term_sums = jnp.dot(attended, grouped_out.T, preferred_element_type=jnp.float32)
    term_sums = term_sums.astype(jnp.bfloat16).reshape(slots, groups, -1).transpose(1, 0, 2)
    term_sums = exchange(term_sums, "tensor")
    attn_output = pl.pallas_call(
        total_kernel,
        out_shape=jax.ShapeDtypeStruct((slots, feature_width // groups), jnp.bfloat16),
        in_specs=[vmem, anywhere],
        compiler_params=pltpu.CompilerParams(vmem_limit_bytes=2 << 20),
        name="total",
    )(term_sums, placed)
    attn_output = attn_output.reshape(step_count, row_count, -1)
    return (attn_output, grouped_qkv.T, grouped_out)


def solution(mesh):
    return jax.shard_map(
        on_device,
        mesh=mesh,
        in_specs=(
            P(None, "dp", None),
            P(),
            P("tensor"),
            P("dp", "tensor", None),
            P("dp", "tensor", None),
            P("dp"),
            P(("dp", "tensor"), None),
            P(("dp", "tensor"), None),
        ),
        out_specs=(P(None, "dp", "tensor"), P(None, "tensor"), P(None, "tensor")),
        check_vma=False,
    )
```

```python
import math

import jax
import jax.numpy as jnp
from jax import lax
from jax.experimental import pallas as pl
from jax.experimental.pallas import tpu as pltpu
from jax.sharding import PartitionSpec as P

HD = 128
QH = 32
KVH = 4
THETA = 1000000.0
EPS = 1e-06
FLOOR = -1e30


def pack_kernel(groups, after_ref, qkv_in, out_in, packed_ref, qkv_ref, out_ref, sems):
    query_width = QH * HD // groups
    kv_width = KVH * HD // groups
    rows = qkv_ref.shape[0]
    quarter = rows // 4
    copies = []
    for i, (source, target) in enumerate(((qkv_in, qkv_ref), (out_in, out_ref))):
        copies.append(pltpu.make_async_copy(source, target, sems.at[i]))
    for copy in copies:
        copy.start()
    for copy in copies:
        copy.wait()
    for g in range(groups):
        keys_at = QH * HD + g * kv_width
        values_at = QH * HD + KVH * HD + g * kv_width
        at = slice(g * query_width, (g + 1) * query_width)
        packed_ref[g, :rows, :] = qkv_ref[:, at]
        packed_ref[g, rows : 2 * rows, :] = out_ref[:, at]
        pair = jnp.concatenate(
            [
                qkv_ref[:, keys_at : keys_at + kv_width],
                qkv_ref[:, values_at : values_at + kv_width],
            ],
            1,
        )
        packed_ref[g, 2 * rows :, :] = jnp.concatenate(
            [pair[i * quarter : (i + 1) * quarter] for i in range(4)], 1
        )


def unpacked(packed_ref):
    groups, rows, query_width = packed_ref.shape
    rows = rows * 4 // 9
    pair_width = query_width // 4
    queries = jnp.concatenate([packed_ref[t, :rows, :] for t in range(groups)], 0)
    pairs = jnp.concatenate(
        [
            packed_ref[t, 2 * rows :, i * pair_width : (i + 1) * pair_width]
            for t in range(groups)
            for i in range(4)
        ],
        0,
    )
    return queries, pairs


def norm_kernel(states_in, gain_in, own_ref, send_ref, states_ref, gain_ref, sems):
    copies = [
        pltpu.make_async_copy(states_in, states_ref, sems.at[0]),
        pltpu.make_async_copy(gain_in, gain_ref, sems.at[1]),
    ]
    for copy in copies:
        copy.start()
    for copy in copies:
        copy.wait()
    states = jnp.concatenate([states_ref[0], states_ref[1]], 0).astype(jnp.float32)
    normed = (
        states
        * lax.rsqrt(jnp.mean(states * states, -1, keepdims=True) + EPS)
        * gain_ref[...].reshape(1, -1).astype(jnp.float32)
    ).astype(jnp.bfloat16)
    replica = lax.axis_index("dp")
    column, y_at = replica // 4, replica % 4
    count, _, share = own_ref.shape
    for y in range(count):
        first = normed[:, y * share : (y + 1) * share]
        second = normed[:, (count + y) * share : (count + y + 1) * share]
        slot = (y - y_at) & 3
        own_ref[slot] = jnp.where(column == 0, first, second)
        send_ref[slot] = jnp.where(column == 0, second, first)


def terms_kernel(own, got, low, high, far, packed_ref, terms_ref, out_ref):
    states = jnp.concatenate(
        [own[0], got[0], low[0], low[1], high[0], high[1], far[0], far[1]], 0
    )
    terms = jnp.concatenate(
        [
            jnp.dot(states, weights, preferred_element_type=jnp.float32)
            for weights in unpacked(packed_ref)
        ],
        1,
    ).astype(terms_ref.dtype)
    slots = own.shape[1]
    replica = lax.axis_index("dp")
    order = [(c, y) for y in (0, -1, 1, 2) for c in (0, 1)]
    for i, (c, y) in enumerate(order):
        source = ((replica // 4) ^ c) * 4 + ((replica + y) & 3)
        terms_ref[source] = terms[i * slots : (i + 1) * slots]
    groups, rows, _ = packed_ref.shape
    rows = rows * 4 // 9
    for t in range(groups):
        out_ref[t * rows : (t + 1) * rows] = packed_ref[t, rows : 2 * rows, :]


def hold_kernel(*refs):
    pass


def hold(*values):
    anywhere = pl.BlockSpec(memory_space=pl.ANY)
    return pl.pallas_call(
        hold_kernel,
        out_shape=tuple(jax.ShapeDtypeStruct(v.shape, v.dtype) for v in values),
        in_specs=[anywhere] * len(values),
        out_specs=(anywhere,) * len(values),
        input_output_aliases={i: i for i in range(len(values))},
        compiler_params=pltpu.CompilerParams(vmem_limit_bytes=1 << 20),
        name="hold",
    )(*values)


def sum_kernel(groups, terms_ref, bias_ref, projected_ref):
    total = jnp.sum(terms_ref[...].astype(jnp.float32), 0) + bias_ref[...].astype(jnp.float32)
    total = total.astype(projected_ref.dtype)
    for g in range(groups):
        projected_ref[g] = total


def turn_kernel(packed_ref, turned_ref):
    queries, pairs = unpacked(packed_ref)
    width = queries.shape[1]
    turned_ref[:width] = queries.T
    turned_ref[width:] = pairs.T


def place_kernel(axis, where, mark, *refs):
    parts = refs[: len(where)]
    replica = lax.axis_index("dp")
    whole_ref, sems = refs[-2:]
    if mark:
        whole_ref, mark_ref, sems = refs[-3:]
        mark_ref[...] = jnp.zeros_like(mark_ref)
    copies = []
    for i, (part, (c, y)) in enumerate(zip(parts, where)):
        size = part.shape[axis]
        source = ((replica // 4) ^ c) * 4 + ((replica + y) & 3)
        at = pl.ds(pl.multiple_of(source * size, size), size)
        target = whole_ref.at[at, :] if axis == 0 else whole_ref.at[:, at]
        copies.append(pltpu.make_async_copy(part, target, sems.at[i]))
    for copy in copies:
        copy.start()
    for copy in copies:
        copy.wait()


def place(whole, parts, where, axis, shape, mark=False):
    count = len(parts)
    continued = whole is not None
    whole_shape = jax.ShapeDtypeStruct(shape, parts[0].dtype)
    vmem = pl.BlockSpec(memory_space=pltpu.VMEM)
    anywhere = pl.BlockSpec(memory_space=pl.ANY)
    return pl.pallas_call(
        lambda *refs: place_kernel(axis, where, mark, *refs),
        out_shape=(whole_shape, jax.ShapeDtypeStruct((8, 128), jnp.float32))
        if mark
        else whole_shape,
        in_specs=[vmem] * count + ([anywhere] if continued else []),
        out_specs=(anywhere, vmem) if mark else anywhere,
        scratch_shapes=[pltpu.SemaphoreType.DMA((count,))],
        input_output_aliases={count: 0} if continued else {},
        compiler_params=pltpu.CompilerParams(vmem_limit_bytes=4 << 20),
        name="place",
    )(*parts, *((whole,) if continued else ()))


def attend_kernel(scale, lengths_ref, cosine_ref, sine_ref, new_ref, key_ref, value_ref, message_ref, query_s, message_s, key_s, value_s, sems):
    groups, slots, _ = new_ref.shape
    rows, span, _ = key_ref.shape
    per_row = 4 * groups
    key_copies, value_copies = (
        [
            pltpu.make_async_copy(
                ref.at[pl.ds(r, 4)], scratch.at[pl.ds(r, 4)], sems.at[i, r]
            )
            for r in range(0, rows, 4)
        ]
        for i, (ref, scratch) in enumerate(((key_ref, key_s), (value_ref, value_s)))
    )
    for copy in key_copies + value_copies:
        copy.start()
    cosine, sine = cosine_ref[...], sine_ref[...]

    def turned(values):
        values = values.astype(jnp.float32)
        return values * cosine + pltpu.roll(values, HD // 2, 1) * sine

    for t in range(groups):
        for j in range(2):
            query = turned(new_ref[t, :, j * HD : (j + 1) * HD])
            for s in range(2):
                query_s[pl.ds(t * 4 + j * 2 + s, rows, stride=per_row), :] = query[
                    s * rows : (s + 1) * rows
                ]
    start, width = 2 * HD, KVH * HD // groups
    new_keys = jnp.concatenate([new_ref[t, :, start : start + width] for t in range(groups)], 1)
    new_keys = jnp.concatenate(
        [turned(new_keys[:, k * HD : (k + 1) * HD]) for k in range(KVH)], 1
    ).astype(jnp.bfloat16)
    new_values = jnp.concatenate(
        [new_ref[t, :, start + width : start + 2 * width] for t in range(groups)], 1
    )

    member = lax.axis_index("tensor")
    total_rows = rows * per_row
    row = lax.broadcasted_iota(jnp.int32, (total_rows, 1), 0)
    kv_of = row[:per_row] // (per_row // KVH)
    position = lax.broadcasted_iota(jnp.int32, (total_rows, span), 1) + member * span
    slot = lax.broadcasted_iota(jnp.int32, (total_rows, slots), 1)
    lane = lax.broadcasted_iota(jnp.int32, (total_rows, HD), 1)

    def product(left, right):
        return lax.dot_general(
            left, right, (((1,), (1,)), ((), ())), preferred_element_type=jnp.float32
        )

    def diagonal(values):
        own = values[:, :HD]
        for k in range(1, KVH):
            own = jnp.where(kv_of == k, values[:, k * HD : (k + 1) * HD], own)
        return own

    def of_row(values, r):
        return values[r * per_row : (r + 1) * per_row]

    queries = []
    for r in range(rows):
        query = query_s[r * per_row : (r + 1) * per_row, :].astype(jnp.bfloat16)
        queries.append(
            jnp.concatenate(
                [jnp.where(kv_of == k, query, jnp.zeros_like(query)) for k in range(KVH)], 1
            )
        )
    fresh = (slot % rows == row // per_row) & (slot // rows <= row % 2) & (member == 0)
    fresh_scores = jnp.where(
        fresh, product(jnp.concatenate(queries, 0), new_keys) * scale, FLOOR
    )
    for copy in key_copies:
        copy.wait()
    scores = jnp.concatenate([product(queries[r], key_s[r]) for r in range(rows)], 0) * scale
    length = jnp.concatenate(
        [jnp.full((per_row, 1), lengths_ref[r], jnp.int32) for r in range(rows)], 0
    )
    valid = position < length
    scores = jnp.where(valid, scores, FLOOR)
    highest = jnp.maximum(
        jnp.max(scores, 1, keepdims=True), jnp.max(fresh_scores, 1, keepdims=True)
    )
    upper = highest.astype(jnp.bfloat16).astype(jnp.float32)
    lower = (highest - upper).astype(jnp.bfloat16).astype(jnp.float32)
    highest = upper + lower
    weights = jnp.where(valid, jnp.exp(scores - highest), 0.0)
    fresh_weights = jnp.where(fresh, jnp.exp(fresh_scores - highest), 0.0)
    total = jnp.sum(weights, 1, keepdims=True) + jnp.sum(fresh_weights, 1, keepdims=True)
    weights = weights.astype(jnp.bfloat16)
    fresh_mixed = jnp.dot(
        fresh_weights.astype(jnp.bfloat16), new_values, preferred_element_type=jnp.float32
    )
    total_upper = total.astype(jnp.bfloat16).astype(jnp.float32)
    total_lower = total - total_upper
    part = lane // 16 % 4
    facts = jnp.where(
        part < 2,
        jnp.where(part == 0, upper, lower),
        jnp.where(part == 2, total_upper, total_lower),
    )
    facts = jnp.where(lane < 64, facts, pltpu.roll(facts, total_rows - 2, 0))
    for copy in value_copies:
        copy.wait()
    for r in range(rows):
        mixed = jnp.dot(of_row(weights, r), value_s[r], preferred_element_type=jnp.float32)
        own = diagonal(mixed + of_row(fresh_mixed, r))
        own_facts = of_row(facts, r)
        for t in range(groups):
            message_s[t, pl.ds(r, 4, stride=rows), :] = own[t * 4 : (t + 1) * 4]
            message_s[t, pl.ds(4 * rows + r, 2, stride=rows), :] = own_facts[t * 4 : t * 4 + 2]
    message_ref[...] = message_s[:, : message_ref.shape[1], :].astype(message_ref.dtype)


def merge_kernel(message_ref, attended_ref):
    message = message_ref[...].astype(jnp.float32)
    half = message.shape[1] * 2 // 3
    facts = message[:, half:]

    def fact(i):
        at = (16 * i, 64 + 16 * i)
        return jnp.concatenate([facts[:, :, lane : lane + 1] for lane in at], 1)

    highest, totals = fact(0) + fact(1), fact(2) + fact(3)
    rescale = jnp.exp(highest - jnp.max(highest, 0, keepdims=True))
    total = jnp.sum(totals * rescale, 0)
    mixture = jnp.sum(message[:, :half] * rescale, 0)
    attended = (mixture / total).astype(attended_ref.dtype)
    attended_ref[...] = jnp.concatenate([attended[: half // 2], attended[half // 2 :]], 1)


def total_kernel(terms_ref, after_ref, output_ref):
    output_ref[...] = jnp.sum(terms_ref[...].astype(jnp.float32), 0).astype(output_ref.dtype)


def exchange(blocks, axis):
    return lax.all_to_all(blocks, axis, split_axis=0, concat_axis=0, tiled=True)


def on_device(hidden, norm_gain, qkv_bias, key_cache, value_cache, lengths, fresh_qkv, fresh_out):
    groups = lax.axis_size("tensor")
    replicas = lax.axis_size("dp")
    step_count, row_count, feature_width = hidden.shape
    slots = step_count * row_count
    share = feature_width // replicas
    query_width = QH * HD // groups
    kv_width = KVH * HD // groups
    own_heads = QH // groups
    score_scale = 1.0 / math.sqrt(HD)

    vmem = pl.BlockSpec(memory_space=pltpu.VMEM)
    smem = pl.BlockSpec(memory_space=pltpu.SMEM)
    anywhere = pl.BlockSpec(memory_space=pl.ANY)
    in_hbm = pl.BlockSpec(memory_space=pltpu.HBM)

    def stay(value):
        return pltpu.with_memory_space_constraint(value, pltpu.HBM)

    across = [(i, i ^ 4) for i in range(replicas)]
    ahead = [(i, (i & 4) | ((i + 1) & 3)) for i in range(replicas)]
    behind = [(i, (i & 4) | ((i + 3) & 3)) for i in range(replicas)]
    beyond = [(i, (i & 4) | ((i + 2) & 3)) for i in range(replicas)]

    def send(value, pairs):
        return lax.ppermute(value, "dp", pairs)

    group_width = query_width + 2 * kv_width
    own_states, other_states = pl.pallas_call(
        norm_kernel,
        out_shape=(jax.ShapeDtypeStruct((replicas // 2, slots, share), jnp.bfloat16),) * 2,
        in_specs=[in_hbm] * 2,
        scratch_shapes=[
            pltpu.VMEM(hidden.shape, hidden.dtype),
            pltpu.VMEM(norm_gain.shape, norm_gain.dtype),
            pltpu.SemaphoreType.DMA((2,)),
        ],
        compiler_params=pltpu.CompilerParams(vmem_limit_bytes=6 << 20),
        name="norm",
    )(stay(hidden), stay(norm_gain))
    cross_states = send(other_states, across)
    packed = pl.pallas_call(
        lambda *refs: pack_kernel(groups, *refs),
        out_shape=jax.ShapeDtypeStruct((groups, fresh_qkv.shape[0] * 9 // 4, query_width), fresh_qkv.dtype),
        in_specs=[anywhere] + [in_hbm] * 2,
        scratch_shapes=[
            pltpu.VMEM(fresh_qkv.shape, fresh_qkv.dtype),
            pltpu.VMEM(fresh_out.shape, fresh_out.dtype),
            pltpu.SemaphoreType.DMA((2,)),
        ],
        compiler_params=pltpu.CompilerParams(vmem_limit_bytes=6 << 20),
        name="pack",
    )(own_states, stay(fresh_qkv), stay(fresh_out))
    packed, cross_states = hold(packed, cross_states)
    packed = exchange(packed, "tensor")

    low_states, far_states, high_states = (
        send(jnp.stack([own_states[k], cross_states[k]]), pairs)
        for k, pairs in ((1, ahead), (2, beyond), (3, behind))
    )
    terms, own_out = pl.pallas_call(
        terms_kernel,
        out_shape=(
            jax.ShapeDtypeStruct((replicas, slots, group_width), jnp.bfloat16),
            jax.ShapeDtypeStruct((share, query_width), packed.dtype),
        ),
        compiler_params=pltpu.CompilerParams(vmem_limit_bytes=8 << 20),
        name="terms",
    )(own_states, cross_states, low_states, high_states, far_states, packed)
    terms = exchange(terms, "dp")
    out_across = send(own_out, across)
    out_low, out_high = send(own_out, ahead), send(own_out, behind)
    own_qkv = pl.pallas_call(
        turn_kernel,
        out_shape=jax.ShapeDtypeStruct((group_width, share), packed.dtype),
        compiler_params=pltpu.CompilerParams(vmem_limit_bytes=4 << 20),
        name="turn",
    )(packed)
    moved = (out_across,)
    projected, out_across = pl.pallas_call(
        lambda terms_ref, bias_ref, *refs: sum_kernel(groups, terms_ref, bias_ref, refs[1]),
        out_shape=(
            jax.ShapeDtypeStruct((groups, slots, group_width), jnp.bfloat16),
            *(jax.ShapeDtypeStruct(v.shape, v.dtype) for v in moved),
        ),
        in_specs=[vmem] * 2 + [in_hbm],
        out_specs=(vmem, in_hbm),
        input_output_aliases={2: 1},
        compiler_params=pltpu.CompilerParams(vmem_limit_bytes=3 << 20),
        name="sum",
    )(terms, qkv_bias.reshape(1, group_width), stay(out_across))
    gathered = exchange(projected, "tensor")

    out_cross_low, out_cross_high = send(out_across, ahead), send(out_across, behind)
    qkv_low, qkv_high = send(own_qkv, ahead), send(own_qkv, behind)
    qkv_across = send(own_qkv, across)

    out_shape, qkv_shape = (feature_width, query_width), (group_width, feature_width)

    half_width = HD // 2
    inverse = THETA ** (-jnp.arange(half_width, dtype=jnp.float32) * 2.0 / HD)
    position = (lengths[None, :] + jnp.arange(step_count, dtype=jnp.int32)[:, None]).astype(
        jnp.float32
    )
    angles = position.reshape(slots, 1) * inverse
    cosine, sine = jnp.cos(angles), jnp.sin(angles)
    cosine = jnp.concatenate([cosine, cosine], 1)
    sine = jnp.concatenate([-sine, sine], 1)

    grouped_out = place(
        None, [own_out, out_across], [(0, 0), (1, 0)], 0, out_shape
    )
    grouped_out = place(
        grouped_out, [out_low, out_high], [(0, -1), (0, 1)], 0, out_shape
    )

    message = pl.pallas_call(
        lambda *refs: attend_kernel(score_scale, *refs),
        out_shape=jax.ShapeDtypeStruct((groups, 3 * slots, HD), jnp.bfloat16),
        in_specs=[smem] + [vmem] * 3 + [in_hbm] * 2,
        scratch_shapes=[
            pltpu.VMEM((slots * QH + 4 * groups, HD), jnp.float32),
            pltpu.VMEM((groups, 4 * slots, HD), jnp.float32),
            pltpu.VMEM(key_cache.shape, key_cache.dtype),
            pltpu.VMEM(value_cache.shape, value_cache.dtype),
            pltpu.SemaphoreType.DMA((2, row_count)),
        ],
        compiler_params=pltpu.CompilerParams(vmem_limit_bytes=14 << 20),
        name="attend",
    )(lengths, cosine, sine, gathered, stay(key_cache), stay(value_cache))
    message, out_cross_low, out_cross_high, qkv_low, qkv_high, qkv_across, grouped_out = hold(
        message, out_cross_low, out_cross_high, qkv_low, qkv_high, qkv_across, grouped_out
    )
    message = exchange(message, "tensor")
    out_far, out_cross_far = send(out_low, ahead), send(out_cross_high, behind)
    qkv_cross_high = send(qkv_high, across)
    grouped_out = place(
        grouped_out,
        [out_cross_low, out_cross_high],
        [(1, -1), (1, 1)],
        0,
        out_shape,
    )
    grouped_qkv = place(
        None, [own_qkv, qkv_across], [(0, 0), (1, 0)], 1, qkv_shape
    )
    attended = pl.pallas_call(
        merge_kernel,
        out_shape=jax.ShapeDtypeStruct((slots, own_heads * HD), jnp.bfloat16),
        compiler_params=pltpu.CompilerParams(vmem_limit_bytes=3 << 20),
        name="merge",
    )(message)
    grouped_out = place(
        grouped_out,
        [out_far, out_cross_far],
        [(0, 2), (1, 2)],
        0,
        out_shape,
    )
    qkv_far, qkv_cross_far = send(qkv_low, ahead), send(qkv_cross_high, behind)
    qkv_cross_low = send(qkv_low, across)
    grouped_qkv = place(
        grouped_qkv,
        [qkv_low, qkv_high, qkv_cross_high],
        [(0, -1), (0, 1), (1, 1)],
        1,
        qkv_shape,
    )
    grouped_qkv, placed = place(
        grouped_qkv,
        [qkv_far, qkv_cross_low, qkv_cross_far],
        [(0, 2), (1, -1), (1, 2)],
        1,
        qkv_shape,
        mark=True,
    )

    term_sums = jnp.dot(attended, grouped_out.T, preferred_element_type=jnp.float32)
    term_sums = term_sums.astype(jnp.bfloat16).reshape(slots, groups, -1).transpose(1, 0, 2)
    term_sums = exchange(term_sums, "tensor")
    attn_output = pl.pallas_call(
        total_kernel,
        out_shape=jax.ShapeDtypeStruct((slots, feature_width // groups), jnp.bfloat16),
        in_specs=[vmem, anywhere],
        compiler_params=pltpu.CompilerParams(vmem_limit_bytes=2 << 20),
        name="total",
    )(term_sums, placed)
    attn_output = attn_output.reshape(step_count, row_count, -1)
    return (attn_output, grouped_qkv.T, grouped_out)


def solution(mesh):
    return jax.shard_map(
        on_device,
        mesh=mesh,
        in_specs=(
            P(None, "dp", None),
            P(),
            P("tensor"),
            P("dp", "tensor", None),
            P("dp", "tensor", None),
            P("dp"),
            P(("dp", "tensor"), None),
            P(("dp", "tensor"), None),
        ),
        out_specs=(P(None, "dp", "tensor"), P(None, "tensor"), P(None, "tensor")),
        check_vma=False,
    )
```

```python
import math

import jax
import jax.numpy as jnp
from jax import lax
from jax.experimental import pallas as pl
from jax.experimental.pallas import tpu as pltpu
from jax.sharding import PartitionSpec as P

HD = 128
QH = 32
KVH = 4
THETA = 1000000.0
EPS = 1e-06
FLOOR = -1e30


def pack_kernel(groups, after_ref, qkv_in, out_in, packed_ref, qkv_ref, out_ref, sems):
    query_width = QH * HD // groups
    kv_width = KVH * HD // groups
    rows = qkv_ref.shape[0]
    quarter = rows // 4
    copies = []
    for i, (source, target) in enumerate(((qkv_in, qkv_ref), (out_in, out_ref))):
        copies.append(pltpu.make_async_copy(source, target, sems.at[i]))
    for copy in copies:
        copy.start()
    for copy in copies:
        copy.wait()
    for g in range(groups):
        keys_at = QH * HD + g * kv_width
        values_at = QH * HD + KVH * HD + g * kv_width
        at = slice(g * query_width, (g + 1) * query_width)
        packed_ref[g, :rows, :] = qkv_ref[:, at]
        packed_ref[g, rows : 2 * rows, :] = out_ref[:, at]
        pair = jnp.concatenate(
            [
                qkv_ref[:, keys_at : keys_at + kv_width],
                qkv_ref[:, values_at : values_at + kv_width],
            ],
            1,
        )
        packed_ref[g, 2 * rows :, :] = jnp.concatenate(
            [pair[i * quarter : (i + 1) * quarter] for i in range(4)], 1
        )


def unpacked(packed_ref):
    groups, rows, query_width = packed_ref.shape
    rows = rows * 4 // 9
    pair_width = query_width // 4
    queries = jnp.concatenate([packed_ref[t, :rows, :] for t in range(groups)], 0)
    pairs = jnp.concatenate(
        [
            packed_ref[t, 2 * rows :, i * pair_width : (i + 1) * pair_width]
            for t in range(groups)
            for i in range(4)
        ],
        0,
    )
    return queries, pairs


def norm_kernel(states_in, gain_in, own_ref, send_ref, states_ref, gain_ref, sems):
    copies = [
        pltpu.make_async_copy(states_in, states_ref, sems.at[0]),
        pltpu.make_async_copy(gain_in, gain_ref, sems.at[1]),
    ]
    for copy in copies:
        copy.start()
    for copy in copies:
        copy.wait()
    states = jnp.concatenate([states_ref[0], states_ref[1]], 0).astype(jnp.float32)
    normed = (
        states
        * lax.rsqrt(jnp.mean(states * states, -1, keepdims=True) + EPS)
        * gain_ref[...].reshape(1, -1).astype(jnp.float32)
    ).astype(jnp.bfloat16)
    replica = lax.axis_index("dp")
    column, y_at = replica // 4, replica % 4
    count, _, share = own_ref.shape
    for y in range(count):
        first = normed[:, y * share : (y + 1) * share]
        second = normed[:, (count + y) * share : (count + y + 1) * share]
        slot = (y - y_at) & 3
        own_ref[slot] = jnp.where(column == 0, first, second)
        send_ref[slot] = jnp.where(column == 0, second, first)


def terms_kernel(own, got, low, high, far, packed_ref, terms_ref, out_ref):
    states = jnp.concatenate(
        [own[0], got[0], low[0], low[1], high[0], high[1], far[0], far[1]], 0
    )
    terms = jnp.concatenate(
        [
            jnp.dot(states, weights, preferred_element_type=jnp.float32)
            for weights in unpacked(packed_ref)
        ],
        1,
    ).astype(terms_ref.dtype)
    slots = own.shape[1]
    replica = lax.axis_index("dp")
    order = [(c, y) for y in (0, -1, 1, 2) for c in (0, 1)]
    for i, (c, y) in enumerate(order):
        source = ((replica // 4) ^ c) * 4 + ((replica + y) & 3)
        terms_ref[source] = terms[i * slots : (i + 1) * slots]
    groups, rows, _ = packed_ref.shape
    rows = rows * 4 // 9
    for t in range(groups):
        out_ref[t * rows : (t + 1) * rows] = packed_ref[t, rows : 2 * rows, :]


def hold_kernel(*refs):
    pass


def hold(*values):
    anywhere = pl.BlockSpec(memory_space=pl.ANY)
    return pl.pallas_call(
        hold_kernel,
        out_shape=tuple(jax.ShapeDtypeStruct(v.shape, v.dtype) for v in values),
        in_specs=[anywhere] * len(values),
        out_specs=(anywhere,) * len(values),
        input_output_aliases={i: i for i in range(len(values))},
        compiler_params=pltpu.CompilerParams(vmem_limit_bytes=1 << 20),
        name="hold",
    )(*values)


def sum_kernel(groups, terms_ref, bias_ref, projected_ref):
    total = jnp.sum(terms_ref[...].astype(jnp.float32), 0) + bias_ref[...].astype(jnp.float32)
    total = total.astype(projected_ref.dtype)
    for g in range(groups):
        projected_ref[g] = total


def turn_kernel(packed_ref, turned_ref):
    queries, pairs = unpacked(packed_ref)
    width = queries.shape[1]
    turned_ref[:width] = queries.T
    turned_ref[width:] = pairs.T


def place_kernel(axis, where, mark, *refs):
    parts = refs[: len(where)]
    replica = lax.axis_index("dp")
    whole_ref, sems = refs[-2:]
    if mark:
        whole_ref, mark_ref, sems = refs[-3:]
        mark_ref[...] = jnp.zeros_like(mark_ref)
    copies = []
    for i, (part, (c, y)) in enumerate(zip(parts, where)):
        size = part.shape[axis]
        source = ((replica // 4) ^ c) * 4 + ((replica + y) & 3)
        at = pl.ds(pl.multiple_of(source * size, size), size)
        target = whole_ref.at[at, :] if axis == 0 else whole_ref.at[:, at]
        copies.append(pltpu.make_async_copy(part, target, sems.at[i]))
    for copy in copies:
        copy.start()
    for copy in copies:
        copy.wait()


def place(whole, parts, where, axis, shape, mark=False):
    count = len(parts)
    continued = whole is not None
    whole_shape = jax.ShapeDtypeStruct(shape, parts[0].dtype)
    vmem = pl.BlockSpec(memory_space=pltpu.VMEM)
    anywhere = pl.BlockSpec(memory_space=pl.ANY)
    return pl.pallas_call(
        lambda *refs: place_kernel(axis, where, mark, *refs),
        out_shape=(whole_shape, jax.ShapeDtypeStruct((8, 128), jnp.float32))
        if mark
        else whole_shape,
        in_specs=[vmem] * count + ([anywhere] if continued else []),
        out_specs=(anywhere, vmem) if mark else anywhere,
        scratch_shapes=[pltpu.SemaphoreType.DMA((count,))],
        input_output_aliases={count: 0} if continued else {},
        compiler_params=pltpu.CompilerParams(vmem_limit_bytes=4 << 20),
        name="place",
    )(*parts, *((whole,) if continued else ()))


def attend_kernel(scale, lengths_ref, cosine_ref, sine_ref, new_ref, key_ref, value_ref, message_ref, query_s, message_s, key_s, value_s, sems):
    groups, slots, _ = new_ref.shape
    rows, span, _ = key_ref.shape
    per_row = 4 * groups
    key_copies, value_copies = (
        [
            pltpu.make_async_copy(
                ref.at[pl.ds(r, 4)], scratch.at[pl.ds(r, 4)], sems.at[i, r]
            )
            for r in range(0, rows, 4)
        ]
        for i, (ref, scratch) in enumerate(((key_ref, key_s), (value_ref, value_s)))
    )
    for copy in key_copies + value_copies:
        copy.start()
    cosine, sine = cosine_ref[...], sine_ref[...]

    def turned(values):
        values = values.astype(jnp.float32)
        return values * cosine + pltpu.roll(values, HD // 2, 1) * sine

    for t in range(groups):
        for j in range(2):
            query = turned(new_ref[t, :, j * HD : (j + 1) * HD])
            for s in range(2):
                query_s[pl.ds(t * 4 + j * 2 + s, rows, stride=per_row), :] = query[
                    s * rows : (s + 1) * rows
                ]
    start, width = 2 * HD, KVH * HD // groups
    new_keys = jnp.concatenate([new_ref[t, :, start : start + width] for t in range(groups)], 1)
    new_keys = jnp.concatenate(
        [turned(new_keys[:, k * HD : (k + 1) * HD]) for k in range(KVH)], 1
    ).astype(jnp.bfloat16)
    new_values = jnp.concatenate(
        [new_ref[t, :, start + width : start + 2 * width] for t in range(groups)], 1
    )

    member = lax.axis_index("tensor")
    total_rows = rows * per_row
    row = lax.broadcasted_iota(jnp.int32, (total_rows, 1), 0)
    kv_of = row[:per_row] // (per_row // KVH)
    position = lax.broadcasted_iota(jnp.int32, (total_rows, span), 1) + member * span
    slot = lax.broadcasted_iota(jnp.int32, (total_rows, slots), 1)
    lane = lax.broadcasted_iota(jnp.int32, (total_rows, HD), 1)

    def product(left, right):
        return lax.dot_general(
            left, right, (((1,), (1,)), ((), ())), preferred_element_type=jnp.float32
        )

    def diagonal(values):
        own = values[:, :HD]
        for k in range(1, KVH):
            own = jnp.where(kv_of == k, values[:, k * HD : (k + 1) * HD], own)
        return own

    def of_row(values, r):
        return values[r * per_row : (r + 1) * per_row]

    queries = []
    for r in range(rows):
        query = query_s[r * per_row : (r + 1) * per_row, :].astype(jnp.bfloat16)
        queries.append(
            jnp.concatenate(
                [jnp.where(kv_of == k, query, jnp.zeros_like(query)) for k in range(KVH)], 1
            )
        )
    fresh = (slot % rows == row // per_row) & (slot // rows <= row % 2) & (member == 0)
    fresh_scores = jnp.where(
        fresh, product(jnp.concatenate(queries, 0), new_keys) * scale, FLOOR
    )
    for copy in key_copies:
        copy.wait()
    scores = jnp.concatenate([product(queries[r], key_s[r]) for r in range(rows)], 0) * scale
    length = jnp.concatenate(
        [jnp.full((per_row, 1), lengths_ref[r], jnp.int32) for r in range(rows)], 0
    )
    valid = position < length
    scores = jnp.where(valid, scores, FLOOR)
    highest = jnp.maximum(
        jnp.max(scores, 1, keepdims=True), jnp.max(fresh_scores, 1, keepdims=True)
    )
    upper = highest.astype(jnp.bfloat16).astype(jnp.float32)
    lower = (highest - upper).astype(jnp.bfloat16).astype(jnp.float32)
    highest = upper + lower
    weights = jnp.where(valid, jnp.exp(scores - highest), 0.0)
    fresh_weights = jnp.where(fresh, jnp.exp(fresh_scores - highest), 0.0)
    total = jnp.sum(weights, 1, keepdims=True) + jnp.sum(fresh_weights, 1, keepdims=True)
    weights = weights.astype(jnp.bfloat16)
    fresh_mixed = jnp.dot(
        fresh_weights.astype(jnp.bfloat16), new_values, preferred_element_type=jnp.float32
    )
    total_upper = total.astype(jnp.bfloat16).astype(jnp.float32)
    total_lower = total - total_upper
    part = lane // 16 % 4
    facts = jnp.where(
        part < 2,
        jnp.where(part == 0, upper, lower),
        jnp.where(part == 2, total_upper, total_lower),
    )
    facts = jnp.where(lane < 64, facts, pltpu.roll(facts, total_rows - 2, 0))
    for copy in value_copies:
        copy.wait()
    for r in range(rows):
        mixed = jnp.dot(of_row(weights, r), value_s[r], preferred_element_type=jnp.float32)
        own = diagonal(mixed + of_row(fresh_mixed, r))
        own_facts = of_row(facts, r)
        for t in range(groups):
            message_s[t, pl.ds(r, 4, stride=rows), :] = own[t * 4 : (t + 1) * 4]
            message_s[t, pl.ds(4 * rows + r, 2, stride=rows), :] = own_facts[t * 4 : t * 4 + 2]
    message_ref[...] = message_s[:, : message_ref.shape[1], :].astype(message_ref.dtype)


def merge_kernel(message_ref, attended_ref):
    message = message_ref[...].astype(jnp.float32)
    half = message.shape[1] * 2 // 3
    facts = message[:, half:]

    def fact(i):
        at = (16 * i, 64 + 16 * i)
        return jnp.concatenate([facts[:, :, lane : lane + 1] for lane in at], 1)

    highest, totals = fact(0) + fact(1), fact(2) + fact(3)
    rescale = jnp.exp(highest - jnp.max(highest, 0, keepdims=True))
    total = jnp.sum(totals * rescale, 0)
    mixture = jnp.sum(message[:, :half] * rescale, 0)
    attended = (mixture / total).astype(attended_ref.dtype)
    attended_ref[...] = jnp.concatenate([attended[: half // 2], attended[half // 2 :]], 1)


def place_and_merge_kernel(where, message_ref, first_ref, second_ref, _, whole_ref, attended_ref, sems):
    replica = lax.axis_index("dp")
    copies = []
    for i, (part, (c, y)) in enumerate(zip((first_ref, second_ref), where)):
        size = part.shape[0]
        source = ((replica // 4) ^ c) * 4 + ((replica + y) & 3)
        target = whole_ref.at[pl.ds(pl.multiple_of(source * size, size), size), :]
        copies.append(pltpu.make_async_copy(part, target, sems.at[i]))
    for copy in copies:
        copy.start()
    merge_kernel(message_ref, attended_ref)
    for copy in copies:
        copy.wait()


def total_kernel(terms_ref, after_ref, output_ref):
    output_ref[...] = jnp.sum(terms_ref[...].astype(jnp.float32), 0).astype(output_ref.dtype)


def exchange(blocks, axis):
    return lax.all_to_all(blocks, axis, split_axis=0, concat_axis=0, tiled=True)


def on_device(hidden, norm_gain, qkv_bias, key_cache, value_cache, lengths, fresh_qkv, fresh_out):
    groups = lax.axis_size("tensor")
    replicas = lax.axis_size("dp")
    step_count, row_count, feature_width = hidden.shape
    slots = step_count * row_count
    share = feature_width // replicas
    query_width = QH * HD // groups
    kv_width = KVH * HD // groups
    own_heads = QH // groups
    score_scale = 1.0 / math.sqrt(HD)

    vmem = pl.BlockSpec(memory_space=pltpu.VMEM)
    smem = pl.BlockSpec(memory_space=pltpu.SMEM)
    anywhere = pl.BlockSpec(memory_space=pl.ANY)
    in_hbm = pl.BlockSpec(memory_space=pltpu.HBM)

    def stay(value):
        return pltpu.with_memory_space_constraint(value, pltpu.HBM)

    across = [(i, i ^ 4) for i in range(replicas)]
    ahead = [(i, (i & 4) | ((i + 1) & 3)) for i in range(replicas)]
    behind = [(i, (i & 4) | ((i + 3) & 3)) for i in range(replicas)]
    beyond = [(i, (i & 4) | ((i + 2) & 3)) for i in range(replicas)]

    def send(value, pairs):
        return lax.ppermute(value, "dp", pairs)

    group_width = query_width + 2 * kv_width
    own_states, other_states = pl.pallas_call(
        norm_kernel,
        out_shape=(jax.ShapeDtypeStruct((replicas // 2, slots, share), jnp.bfloat16),) * 2,
        in_specs=[in_hbm] * 2,
        scratch_shapes=[
            pltpu.VMEM(hidden.shape, hidden.dtype),
            pltpu.VMEM(norm_gain.shape, norm_gain.dtype),
            pltpu.SemaphoreType.DMA((2,)),
        ],
        compiler_params=pltpu.CompilerParams(vmem_limit_bytes=6 << 20),
        name="norm",
    )(stay(hidden), stay(norm_gain))
    cross_states = send(other_states, across)
    packed = pl.pallas_call(
        lambda *refs: pack_kernel(groups, *refs),
        out_shape=jax.ShapeDtypeStruct((groups, fresh_qkv.shape[0] * 9 // 4, query_width), fresh_qkv.dtype),
        in_specs=[anywhere] + [in_hbm] * 2,
        scratch_shapes=[
            pltpu.VMEM(fresh_qkv.shape, fresh_qkv.dtype),
            pltpu.VMEM(fresh_out.shape, fresh_out.dtype),
            pltpu.SemaphoreType.DMA((2,)),
        ],
        compiler_params=pltpu.CompilerParams(vmem_limit_bytes=6 << 20),
        name="pack",
    )(own_states, stay(fresh_qkv), stay(fresh_out))
    packed, cross_states = hold(packed, cross_states)
    packed = exchange(packed, "tensor")

    low_states, far_states, high_states = (
        send(jnp.stack([own_states[k], cross_states[k]]), pairs)
        for k, pairs in ((1, ahead), (2, beyond), (3, behind))
    )
    terms, own_out = pl.pallas_call(
        terms_kernel,
        out_shape=(
            jax.ShapeDtypeStruct((replicas, slots, group_width), jnp.bfloat16),
            jax.ShapeDtypeStruct((share, query_width), packed.dtype),
        ),
        compiler_params=pltpu.CompilerParams(vmem_limit_bytes=8 << 20),
        name="terms",
    )(own_states, cross_states, low_states, high_states, far_states, packed)
    terms = exchange(terms, "dp")
    out_across = send(own_out, across)
    out_low, out_high = send(own_out, ahead), send(own_out, behind)
    own_qkv = pl.pallas_call(
        turn_kernel,
        out_shape=jax.ShapeDtypeStruct((group_width, share), packed.dtype),
        compiler_params=pltpu.CompilerParams(vmem_limit_bytes=4 << 20),
        name="turn",
    )(packed)
    moved = (out_across,)
    projected, out_across = pl.pallas_call(
        lambda terms_ref, bias_ref, *refs: sum_kernel(groups, terms_ref, bias_ref, refs[1]),
        out_shape=(
            jax.ShapeDtypeStruct((groups, slots, group_width), jnp.bfloat16),
            *(jax.ShapeDtypeStruct(v.shape, v.dtype) for v in moved),
        ),
        in_specs=[vmem] * 2 + [in_hbm],
        out_specs=(vmem, in_hbm),
        input_output_aliases={2: 1},
        compiler_params=pltpu.CompilerParams(vmem_limit_bytes=3 << 20),
        name="sum",
    )(terms, qkv_bias.reshape(1, group_width), stay(out_across))
    gathered = exchange(projected, "tensor")

    out_cross_low, out_cross_high = send(out_across, ahead), send(out_across, behind)
    qkv_low, qkv_high = send(own_qkv, ahead), send(own_qkv, behind)
    qkv_across = send(own_qkv, across)

    out_shape, qkv_shape = (feature_width, query_width), (group_width, feature_width)

    half_width = HD // 2
    inverse = THETA ** (-jnp.arange(half_width, dtype=jnp.float32) * 2.0 / HD)
    position = (lengths[None, :] + jnp.arange(step_count, dtype=jnp.int32)[:, None]).astype(
        jnp.float32
    )
    angles = position.reshape(slots, 1) * inverse
    cosine, sine = jnp.cos(angles), jnp.sin(angles)
    cosine = jnp.concatenate([cosine, cosine], 1)
    sine = jnp.concatenate([-sine, sine], 1)

    grouped_out = place(
        None, [own_out, out_across], [(0, 0), (1, 0)], 0, out_shape
    )
    grouped_out = place(
        grouped_out, [out_low, out_high], [(0, -1), (0, 1)], 0, out_shape
    )

    message = pl.pallas_call(
        lambda *refs: attend_kernel(score_scale, *refs),
        out_shape=jax.ShapeDtypeStruct((groups, 3 * slots, HD), jnp.bfloat16),
        in_specs=[smem] + [vmem] * 3 + [in_hbm] * 2,
        scratch_shapes=[
            pltpu.VMEM((slots * QH + 4 * groups, HD), jnp.float32),
            pltpu.VMEM((groups, 4 * slots, HD), jnp.float32),
            pltpu.VMEM(key_cache.shape, key_cache.dtype),
            pltpu.VMEM(value_cache.shape, value_cache.dtype),
            pltpu.SemaphoreType.DMA((2, row_count)),
        ],
        compiler_params=pltpu.CompilerParams(vmem_limit_bytes=14 << 20),
        name="attend",
    )(lengths, cosine, sine, gathered, stay(key_cache), stay(value_cache))
    message, out_cross_low, out_cross_high, qkv_low, qkv_high, qkv_across, grouped_out = hold(
        message, out_cross_low, out_cross_high, qkv_low, qkv_high, qkv_across, grouped_out
    )
    message = exchange(message, "tensor")
    out_far, out_cross_far = send(out_low, ahead), send(out_cross_high, behind)
    qkv_cross_high = send(qkv_high, across)
    grouped_out = place(
        grouped_out,
        [out_cross_low, out_cross_high],
        [(1, -1), (1, 1)],
        0,
        out_shape,
    )
    grouped_qkv = place(
        None, [own_qkv, qkv_across], [(0, 0), (1, 0)], 1, qkv_shape
    )
    far = ((0, 2), (1, 2))
    grouped_out, attended = pl.pallas_call(
        lambda *refs: place_and_merge_kernel(far, *refs),
        out_shape=(
            jax.ShapeDtypeStruct(out_shape, out_far.dtype),
            jax.ShapeDtypeStruct((slots, own_heads * HD), jnp.bfloat16),
        ),
        in_specs=[vmem] * 3 + [anywhere],
        out_specs=(anywhere, vmem),
        scratch_shapes=[pltpu.SemaphoreType.DMA((2,))],
        input_output_aliases={3: 0},
        compiler_params=pltpu.CompilerParams(vmem_limit_bytes=6 << 20),
        name="place_and_merge",
    )(message, out_far, out_cross_far, grouped_out)
    qkv_far, qkv_cross_far = send(qkv_low, ahead), send(qkv_cross_high, behind)
    qkv_cross_low = send(qkv_low, across)
    grouped_qkv = place(
        grouped_qkv,
        [qkv_low, qkv_high, qkv_cross_high],
        [(0, -1), (0, 1), (1, 1)],
        1,
        qkv_shape,
    )
    grouped_qkv, placed = place(
        grouped_qkv,
        [qkv_far, qkv_cross_low, qkv_cross_far],
        [(0, 2), (1, -1), (1, 2)],
        1,
        qkv_shape,
        mark=True,
    )

    term_sums = jnp.dot(attended, grouped_out.T, preferred_element_type=jnp.float32)
    term_sums = term_sums.astype(jnp.bfloat16).reshape(slots, groups, -1).transpose(1, 0, 2)
    term_sums = exchange(term_sums, "tensor")
    attn_output = pl.pallas_call(
        total_kernel,
        out_shape=jax.ShapeDtypeStruct((slots, feature_width // groups), jnp.bfloat16),
        in_specs=[vmem, anywhere],
        compiler_params=pltpu.CompilerParams(vmem_limit_bytes=2 << 20),
        name="total",
    )(term_sums, placed)
    attn_output = attn_output.reshape(step_count, row_count, -1)
    return (attn_output, grouped_qkv.T, grouped_out)


def solution(mesh):
    return jax.shard_map(
        on_device,
        mesh=mesh,
        in_specs=(
            P(None, "dp", None),
            P(),
            P("tensor"),
            P("dp", "tensor", None),
            P("dp", "tensor", None),
            P("dp"),
            P(("dp", "tensor"), None),
            P(("dp", "tensor"), None),
        ),
        out_specs=(P(None, "dp", "tensor"), P(None, "tensor"), P(None, "tensor")),
        check_vma=False,
    )
```
